32 devices in a mesh: dp: 8 (over y, x, core), mp: 4 (over z).
Axes of the slice: x: 2, y: 2, z: 4, core: 2. Of those that a mesh axis runs over, the one named last changes fastest.
Arguments:
- byte_ids: int32 [16384], P(('dp', 'mp')), may hold values from 0 to 255
- embed_table: bfloat16 [256, 512], replicated, may hold values from -6 to 6
- boundary_labels: int32 [16384], P('dp'), may hold values 0 or 1
- out_cotangent: bfloat16 [16384, 512], P(('dp', 'mp')), may hold values from -6 to 6
- norm_one_gain: bfloat16 [512], replicated, may hold values from 0.5 to 1.5
- norm_one_bias: bfloat16 [512], replicated, may hold values from -2 to 2
- w_query: bfloat16 [512, 512], P(None, 'mp'), may hold values from -0.25 to 0.25
- w_key: bfloat16 [512, 512], P(None, 'mp'), may hold values from -0.25 to 0.25
- w_value: bfloat16 [512, 512], P(None, 'mp'), may hold values from -0.25 to 0.25
- w_position: bfloat16 [512, 512], P(None, 'mp'), may hold values from -0.25 to 0.25
- content_bias: bfloat16 [8, 64], P('mp'), may hold values from -3 to 3
- position_bias: bfloat16 [8, 64], P('mp'), may hold values from -3 to 3
- w_out: bfloat16 [512, 512], P('mp'), may hold values from -0.75 to 0.75
- norm_two_gain: bfloat16 [512], replicated, may hold values from 0.5 to 1.5
- norm_two_bias: bfloat16 [512], replicated, may hold values from -2 to 2
- w_up: bfloat16 [512, 2048], P(None, 'mp'), may hold values from -0.25 to 0.25
- up_bias: bfloat16 [2048], P('mp'), may hold values from -2 to 2
- w_down: bfloat16 [2048, 512], P('mp'), may hold values from -0.125 to 0.125
- down_bias: bfloat16 [512], replicated, may hold values from -2 to 2
- w_pred: bfloat16 [512, 2048], P(None, 'mp'), may hold values from -0.25 to 0.25
- pred_bias: bfloat16 [2048], P('mp'), may hold values from -2 to 2
- w_logit: bfloat16 [2048], P('mp'), may hold values from -0.5 to 0.5
- logit_bias: bfloat16 [1], replicated, may hold values from -1 to 1
Outputs:
- block_out: bfloat16 [16384, 512], P(('dp', 'mp'))
- loss_value: float32 [1], replicated
- grad_input: bfloat16 [16384, 512], P(('dp', 'mp'))
- grad_embed: float32 [256, 512], replicated
- grad_norm_one_gain: float32 [512], replicated
- grad_norm_one_bias: float32 [512], replicated
- grad_w_query: float32 [512, 512], P(None, 'mp')
- grad_w_key: float32 [512, 512], P(None, 'mp')
- grad_w_value: float32 [512, 512], P(None, 'mp')
- grad_w_position: float32 [512, 512], P(None, 'mp')
- grad_content_bias: float32 [8, 64], P('mp')
- grad_position_bias: float32 [8, 64], P('mp')
- grad_w_out: float32 [512, 512], P('mp')
- grad_norm_two_gain: float32 [512], replicated
- grad_norm_two_bias: float32 [512], replicated
- grad_w_up: float32 [512, 2048], P(None, 'mp')
- grad_up_bias: float32 [2048], P('mp')
- grad_w_down: float32 [2048, 512], P('mp')
- grad_down_bias: float32 [512], replicated
- grad_w_pred: float32 [512, 2048], P(None, 'mp')
- grad_pred_bias: float32 [2048], P('mp')
- grad_w_logit: float32 [2048], P('mp')
- grad_logit_bias: float32 [1], replicated
The draws below stay inside these ranges and needn't reach their ends.
All inputs are finite; a program needn't handle non-finite values. No bound on the sum of `boundary_labels` on one device may be relied on, other than what follows from the above.
Results may differ from the reference program's by a relative error of at most 0.025.
Values may be sent and summed in bfloat16 or wider, within the bound.
No kernel may reach another device: no remote copies, remote signals or barrier semaphores. Data moves between devices by JAX's collectives and lax.ppermute only.
A program may use at most 192 MiB of HBM per device.

```python
import math
import jax
import jax.numpy as jnp
import numpy as np
from jax import lax

D = 512
HEADS = 8
HD = 64
FF = 2048
VOCAB = 256
LEN = 2048
TOKENS = 16384


def with_ends(result, own_key, least, top_value):
    extent = result.shape
    place = [jax.random.randint(jax.random.fold_in(own_key, axis), (), 0, extent[axis]) for axis in range(len(extent))]
    result = result.at[tuple(place)].set(least)
    longest = extent.index(max(extent))
    place[longest] = (place[longest] + 1) % extent[longest]
    return result.at[tuple(place)].set(top_value)


def block_levels(own_key, extent, split, least, top_value):
    def one(position, parts):
        steps = jax.random.uniform(jax.random.fold_in(jax.random.fold_in(own_key, 6), position), (parts,), jnp.float32, least / len(split), top_value / len(split))
        return jnp.repeat(jnp.exp(steps), extent[position] // parts).reshape((-1,) + (1,) * (len(extent) - position - 1))

    level = one(*split[0])
    for cut in split[1:]:
        level = level * one(*cut)
    return level


def cumulative_ranks(count, slope):
    weights = [(1 << 20) // math.isqrt(rank ** slope) + 1 for rank in range(1, count + 1)]
    width = 1 + sum(weights) // (1 << 30)
    return np.cumsum(np.array([max(1, weight // width) for weight in weights]))


def ranked_ids(own_key, extent, count, lean):
    table = cumulative_ranks(count, lean)
    ticket = jax.random.randint(jax.random.fold_in(own_key, 1), extent, 0, int(table[count - 1]))
    standing = jnp.searchsorted(jnp.asarray(table, jnp.int32), ticket, side="right")
    return jax.random.permutation(jax.random.fold_in(own_key, 2), count)[standing].astype(jnp.int32)


def bell_draw(rng, dims, width, most, cuts=(), kind=jnp.bfloat16):
    entries = jax.random.normal(rng, dims, jnp.float32) * width
    if len(cuts) > 0:
        entries = block_levels(rng, dims, cuts, -0.22, 0.18) * entries
    return jnp.clip(entries, min=-most, max=most).astype(kind)


def setup_inputs(seed: int = 0) -> dict:
    splits = jax.random.split(jax.random.key(seed), 24)
    return {
        "byte_ids": with_ends(ranked_ids(splits[0], (TOKENS,), VOCAB, 2), jax.random.fold_in(splits[0], 3), 0, VOCAB - 1).astype(jnp.int32),
        "embed_table": bell_draw(splits[1], (VOCAB, D), 1.0, 6.0),
        "boundary_labels": with_ends((jax.random.randint(splits[2], (TOKENS,), 0, 4) < 1).astype(jnp.int32), jax.random.fold_in(splits[2], 1), 0, 1),
        "out_cotangent": bell_draw(splits[3], (TOKENS, D), 1.0, 6.0, ((0, 32),)),
        "norm_one_gain": jnp.clip(1.0 + 0.1 * jax.random.normal(splits[4], (D,), jnp.float32), 0.5, 1.5).astype(jnp.bfloat16),
        "norm_one_bias": bell_draw(splits[5], (D,), 0.3, 2.0),
        "w_query": bell_draw(splits[6], (D, D), D ** -0.5, 0.25, ((1, 4),)),
        "w_key": bell_draw(splits[7], (D, D), D ** -0.5, 0.25, ((1, 4),)),
        "w_value": bell_draw(splits[8], (D, D), D ** -0.5, 0.25, ((1, 4),)),
        "w_position": bell_draw(splits[9], (D, D), D ** -0.5, 0.25, ((1, 4),)),
        "content_bias": bell_draw(splits[10], (HEADS, HD), 0.5, 3.0, ((0, 4),)),
        "position_bias": bell_draw(splits[11], (HEADS, HD), 0.5, 3.0, ((0, 4),)),
        "w_out": bell_draw(splits[12], (D, D), HD ** -0.5, 0.75, ((0, 4),)),
        "norm_two_gain": jnp.clip(1.0 + 0.1 * jax.random.normal(splits[13], (D,), jnp.float32), 0.5, 1.5).astype(jnp.bfloat16),
        "norm_two_bias": bell_draw(splits[14], (D,), 0.3, 2.0),
        "w_up": bell_draw(splits[15], (D, FF), D ** -0.5, 0.25, ((1, 4),)),
        "up_bias": bell_draw(splits[16], (FF,), 0.3, 2.0, ((0, 4),)),
        "w_down": bell_draw(splits[17], (FF, D), FF ** -0.5, 0.125, ((0, 4),)),
        "down_bias": bell_draw(splits[18], (D,), 0.3, 2.0),
        "w_pred": bell_draw(splits[19], (D, FF), D ** -0.5, 0.25, ((1, 4),)),
        "pred_bias": bell_draw(splits[20], (FF,), 0.3, 2.0, ((0, 4),)),
        "w_logit": bell_draw(splits[21], (FF,), 128 ** -0.5, 0.5, ((0, 4),)),
        "logit_bias": jnp.clip(jax.random.uniform(splits[22], (1,), jnp.float32, -1.0, 1.0), -1.0, 1.0).astype(jnp.bfloat16),
    }


@jax.custom_vjp
def low(v):
    return lax.optimization_barrier(v.astype(jnp.bfloat16)).astype(jnp.float32)

@jax.custom_vjp
def low_back(v):
    return v

def low_keep(v):
    return (low(v), None)

def low_pass(kept, grad):
    return (grad,)

def back_keep(v):
    return (v, None)

def back_low(kept, grad):
    return (low(grad),)
low.defvjp(low_keep, low_pass)
low_back.defvjp(back_keep, back_low)

def normalize(values, gain_row, shift_row):
    centered = values - lax.optimization_barrier(jnp.mean(values, axis=-1, keepdims=True))
    return centered * lax.rsqrt(lax.optimization_barrier(jnp.mean(centered * centered, axis=-1, keepdims=True)) + 1e-05) * gain_row + shift_row

def matmul(first_mat, second_mat):
    return jnp.dot(first_mat, second_mat, precision=lax.Precision.HIGHEST)

def rotation_tables():
    frequency = jnp.exp(jnp.arange(D // 2, dtype=jnp.float32) * (-2.0 * math.log(10000.0) / D))
    angles = jnp.arange(LEN, dtype=jnp.float32)[:, None] * frequency[None, :]
    return (jnp.sin(angles), jnp.cos(angles))

def sequence_layer(inputs, labels, params):
    gain_one, shift_one, query_weight, key_weight, value_weight, position_weight, content_shift, position_shift, output_weight, gain_two, shift_two, up_weight, up_shift, down_weight, down_shift, pred_weight, pred_shift, logit_weight, logit_shift = params
    highest = lax.Precision.HIGHEST
    norm_in = low(normalize(inputs, gain_one, shift_one))
    query_raw = low_back(matmul(norm_in, query_weight))
    query_content = low(query_raw + content_shift.reshape(D)).reshape(LEN, HEADS, HD)
    query_shift = low(query_raw + position_shift.reshape(D)).reshape(LEN, HEADS, HD)
    key_rows = low(low_back(matmul(norm_in, key_weight))).reshape(LEN, HEADS, HD)
    value_rows = low(low_back(matmul(norm_in, value_weight))).reshape(LEN, HEADS, HD)
    coeffs = low_back(jnp.einsum('the,mhe->thm', query_shift, position_weight.reshape(D, HEADS, HD), precision=highest))
    sines, cosines = rotation_tables()
    sine_rows = sines[:, None, :]
    cosine_rows = cosines[:, None, :]
    coeff_sin = coeffs[:, :, :D // 2]
    coeff_cos = coeffs[:, :, D // 2:]
    pos_query = low(jnp.concatenate([coeff_sin * sine_rows + coeff_cos * cosine_rows, coeff_cos * sine_rows - coeff_sin * cosine_rows], axis=-1))
    key_feature = low(jnp.concatenate([cosines, sines], axis=-1))
    scores = jnp.einsum('qhe,khe->hqk', query_content, key_rows, precision=highest)
    scores = scores + jnp.einsum('qhm,km->hqk', pos_query, key_feature, precision=highest)
    scores = low_back(scores * (1.0 / math.sqrt(HD)))
    places = jnp.arange(LEN)
    scores = jnp.where(places[:, None] >= places[None, :], scores, -1000000000.0)
    attention = low(jax.nn.softmax(scores, axis=-1))
    attended = low(low_back(jnp.einsum('hqk,khe->qhe', attention, value_rows, precision=highest))).reshape(LEN, D)
    middle = inputs + low_back(matmul(attended, output_weight))
    norm_mid = low(normalize(middle, gain_two, shift_two))
    up_pre = low_back(matmul(norm_mid, up_weight)) + up_shift
    hidden = low(jax.nn.gelu(up_pre, approximate=False))
    outputs = middle + low_back(matmul(hidden, down_weight)) + down_shift
    out_low = low(outputs)
    pred_pre = low_back(matmul(out_low, pred_weight)) + pred_shift
    pred_hidden = low(jax.nn.gelu(pred_pre, approximate=False))
    logits = low_back(matmul(pred_hidden, logit_weight)) + logit_shift[0]
    losses = jnp.sum(jax.nn.softplus(logits) - labels * logits)
    return (outputs, losses)

def reference(byte_ids, embed_table, boundary_labels, out_cotangent, norm_one_gain, norm_one_bias, w_query, w_key, w_value, w_position, content_bias, position_bias, w_out, norm_two_gain, norm_two_bias, w_up, up_bias, w_down, down_bias, w_pred, pred_bias, w_logit, logit_bias):
    params = tuple((member.astype(jnp.float32) for member in (norm_one_gain, norm_one_bias, w_query, w_key, w_value, w_position, content_bias, position_bias, w_out, norm_two_gain, norm_two_bias, w_up, up_bias, w_down, down_bias, w_pred, pred_bias, w_logit, logit_bias)))
    embed_float = embed_table.astype(jnp.float32)
    seq_count = TOKENS // LEN
    inputs = embed_float[byte_ids].reshape(seq_count, LEN, D)
    labels = boundary_labels.astype(jnp.float32).reshape(seq_count, LEN)
    cotangent = out_cotangent.astype(jnp.float32).reshape(seq_count, LEN, D)

    def one_sequence(running, pieces):
        totals, loss_sum = running
        seq_inputs, seq_labels, seq_cotangent = pieces

        def forward(values, weights):
            return sequence_layer(values, seq_labels, weights)
        (outputs, losses), pullback = jax.vjp(forward, seq_inputs, params)
        grad_in, grad_weights = pullback((seq_cotangent, jnp.ones((), jnp.float32)))
        totals = jax.tree.map(lambda first_term, second_term: first_term + second_term, totals, grad_weights)
        return ((totals, loss_sum + losses), (outputs.astype(jnp.bfloat16), grad_in))
    initial = (jax.tree.map(jnp.zeros_like, params), jnp.zeros((), jnp.float32))
    (totals, loss_sum), (outputs, grad_inputs) = lax.scan(one_sequence, initial, (inputs, labels, cotangent))
    grad_inputs = grad_inputs.reshape(TOKENS, D)
    _, lookup_back = jax.vjp(lambda table_rows: table_rows[byte_ids], embed_float)
    grad_embed, = lookup_back(grad_inputs)
    loss_value = (loss_sum / TOKENS).reshape(1)
    return (outputs.reshape(TOKENS, D), loss_value, grad_inputs.astype(jnp.bfloat16), grad_embed) + tuple(totals)
```

```python
import functools
import math

import jax
import jax.numpy as jnp
import numpy as np
from jax import lax
from jax.experimental import pallas as pl
from jax.experimental.pallas import tpu as pltpu
from jax.sharding import PartitionSpec as P

LEN = 2048
BLOCK = 256
VMEM_BYTES = 56 * 1024 * 1024

bf16 = jnp.bfloat16
f32 = jnp.float32
norm_eps = 1e-05
density_scale = 1.0 / math.sqrt(2.0 * math.pi)
log2_e = math.log2(math.e)


def nn(first, second):
    return jnp.dot(first, second, preferred_element_type=f32)


def nt(first, second):
    return lax.dot_general(
        first, second, (((1,), (1,)), ((), ())), preferred_element_type=f32
    )


def tn(first, second):
    return lax.dot_general(
        first, second, (((0,), (0,)), ((), ())), preferred_element_type=f32
    )


def layer_stats(values):
    centered = values - jnp.mean(values, axis=-1, keepdims=True)
    inverse = lax.rsqrt(jnp.mean(centered * centered, axis=-1, keepdims=True) + norm_eps)
    return centered * inverse, inverse


def norm_back(grad_normed, normed, inverse, gain_row):
    scaled = grad_normed * gain_row
    first_mean = jnp.mean(scaled, axis=-1, keepdims=True)
    second_mean = jnp.mean(scaled * normed, axis=-1, keepdims=True)
    return inverse * (scaled - first_mean - normed * second_mean)


def gelu_parts(values):
    size = jnp.abs(values)
    fall = jnp.exp(-0.5 * values * values)
    t = 1.0 / (1.0 + (0.3275911 / math.sqrt(2.0)) * size)
    poly = 1.061405429 * t - 1.453152027
    poly = poly * t + 1.421413741
    poly = poly * t - 0.284496736
    poly = poly * t + 0.254829592
    tail = 0.5 * poly * t * fall
    phi = jnp.where(values >= 0, 1.0 - tail, tail)
    return values * phi, phi + values * fall * density_scale


def feature_tables(model_width):
    half = model_width // 2
    frequency = np.exp(
        np.arange(half, dtype=np.float64) * (-2.0 * math.log(10000.0) / model_width)
    )
    angles = np.arange(LEN, dtype=np.float64)[:, None] * frequency[None, :]
    return np.sin(angles).astype(np.float32), np.cos(angles).astype(np.float32)


def embed_rows(ids_row, table):
    vocab = table.shape[0]
    places = lax.broadcasted_iota(jnp.int32, (vocab, ids_row.shape[1]), 0)
    one_hot_t = (places == ids_row).astype(f32)
    rows = nn(one_hot_t.T.astype(bf16), table)
    return one_hot_t, rows


def full(shape):
    return pl.BlockSpec(shape, lambda *_: (0,) * len(shape))


def params():
    return pltpu.CompilerParams(vmem_limit_bytes=VMEM_BYTES)


def pre_kernel(mp, heads, score_scale, me_ref, *refs):
    id_refs = refs[:mp]
    (table, gain, bias, w_joint, w_pos, c_bias, p_bias, feature, feature_t, sines, cosines) = refs[
        mp : mp + 11
    ]
    norm_out, qcat, kcat, kcat_t, v_out, v_t, shift_out, ids_s = refs[mp + 11 :]
    step = pl.program_id(0)
    me = me_ref[0]
    own = id_refs[0].shape[1]

    @pl.when(step == 0)
    def _():
        for k in range(mp):
            source = lax.rem(me - k + mp, mp)
            ids_s[:, pl.ds(pl.multiple_of(source * own, own), own)] = id_refs[k][...]

    rows = norm_out.shape[0]
    ids = ids_s[:, pl.ds(pl.multiple_of(step * rows, rows), rows)]
    _, inputs = embed_rows(ids, table[...])
    normed, _ = layer_stats(inputs)
    norm_in = (normed * gain[...] + bias[...]).astype(bf16)
    norm_out[...] = norm_in
    joint = nn(norm_in, w_joint[...])
    width = v_out.shape[1]
    head_size = width // heads
    raw = joint[:, :width]
    keys = joint[:, width : 2 * width].astype(bf16)
    values = joint[:, 2 * width :].astype(bf16)
    v_out[...] = values
    v_t[...] = values.astype(f32).T.astype(bf16)
    model = feature.shape[1]
    half = model // 2
    kcat[:, :model] = feature[...]
    kcat[:, model:] = keys
    keys_t = keys.astype(f32).T.astype(bf16)
    kcat_t[:head_size] = keys_t[:head_size]
    kcat_t[head_size : head_size + model] = feature_t[...]
    if heads > 1:
        kcat_t[head_size + model :] = keys_t[head_size:]
    shift = (raw + p_bias[...]).astype(bf16)
    shift_out[...] = shift
    fold = score_scale * log2_e
    content = (raw + c_bias[...]) * fold
    lane = lax.broadcasted_iota(jnp.int32, content.shape, 1)
    sin, cos = sines[...], cosines[...]
    for h in range(heads):
        low, high = h * head_size, (h + 1) * head_size
        coeffs = nt(shift[:, low:high], w_pos[:, low:high])
        c_sin, c_cos = coeffs[:, :half] * fold, coeffs[:, half:] * fold
        qcat[h, :, :half] = (c_sin * sin + c_cos * cos).astype(bf16)
        qcat[h, :, half:model] = (c_cos * sin - c_sin * cos).astype(bf16)
        mine = (lane >= low) & (lane < high)
        qcat[h, :, model:] = jnp.where(mine, content, 0.0).astype(bf16)


def pre_call(me, id_parts, table, gain, bias, w_joint, w_pos, c_bias, p_bias, tables, heads, scale):
    mp = len(id_parts)
    own = id_parts[0].shape[1]
    model = table.shape[1]
    width = w_pos.shape[1]
    rows = BLOCK
    feature, feature_t, sines, cosines = tables
    cat = model + width
    row_block = lambda n: pl.BlockSpec((rows, n), lambda i, m: (i, 0))
    col_block = lambda n: pl.BlockSpec((n, rows), lambda i, m: (0, i))
    ins = [*id_parts, table, gain, bias, w_joint, w_pos, c_bias, p_bias]
    return pl.pallas_call(
        functools.partial(pre_kernel, mp, heads, scale),
        grid_spec=pltpu.PrefetchScalarGridSpec(
            num_scalar_prefetch=1,
            grid=(LEN // rows,),
            in_specs=[full(a.shape) for a in ins]
            + [row_block(model), col_block(model), row_block(model // 2), row_block(model // 2)],
            out_specs=[
                row_block(model),
                pl.BlockSpec((heads, rows, cat), lambda i, m: (0, i, 0)),
                row_block(cat),
                col_block(cat),
                row_block(width),
                col_block(width),
                row_block(width),
            ],
            scratch_shapes=[pltpu.VMEM((1, mp * own), jnp.int32)],
        ),
        out_shape=[
            jax.ShapeDtypeStruct((LEN, model), bf16),
            jax.ShapeDtypeStruct((heads, LEN, cat), bf16),
            jax.ShapeDtypeStruct((LEN, cat), bf16),
            jax.ShapeDtypeStruct((cat, LEN), bf16),
            jax.ShapeDtypeStruct((LEN, width), bf16),
            jax.ShapeDtypeStruct((width, LEN), bf16),
            jax.ShapeDtypeStruct((LEN, width), bf16),
        ],
        compiler_params=params(),
        cost_estimate=pl.CostEstimate(
            flops=2 * LEN * model * (table.shape[0] + 4 * width), bytes_accessed=24 << 20, transcendentals=0
        ),
        name="project",
    )(me, *ins, feature, feature_t, sines, cosines)


def fwd_kernel(mp, own, me_ref, qcat, kcat, v_t, expon_out, full_t, inv_out, *piece_refs):
    step = pl.program_id(0)
    me = me_ref[0]
    rows = qcat.shape[1]
    for block in range(LEN // rows):

        @pl.when(step == block)
        def _(block=block):
            low, high = block * rows, (block + 1) * rows
            queries = qcat[0]
            last = nt(kcat[low:high], queries)
            key_place = lax.broadcasted_iota(jnp.int32, last.shape, 0)
            query_place = lax.broadcasted_iota(jnp.int32, last.shape, 1)
            last = jnp.where(key_place <= query_place, last, -1e30)
            top = jnp.max(last, axis=0, keepdims=True)
            if block:
                first = nt(kcat[:low], queries)
                top = jnp.maximum(top, jnp.max(first, axis=0, keepdims=True))
            e_last = jnp.exp2(last - top)
            total = jnp.sum(e_last, axis=0, keepdims=True)
            e_last = e_last.astype(bf16)
            expon_out[0, low:high] = e_last
            mixed = nn(v_t[:, low:high], e_last)
            if block:
                e_first = jnp.exp2(first - top)
                total = total + jnp.sum(e_first, axis=0, keepdims=True)
                e_first = e_first.astype(bf16)
                expon_out[0, :low] = e_first
                mixed = mixed + nn(v_t[:, :low], e_first)
            inverse = 1.0 / total
            inv_out[...] = inverse
            mixed = mixed * inverse
            full_t[...] = mixed
            relative = lax.rem(low // own - me + mp, mp)
            start = low % own
            for k in range(mp):

                @pl.when(relative == k)
                def _(k=k):
                    piece_refs[k][:, start : start + rows] = mixed.astype(bf16)


def fwd_call(me, head, qcat, kcat, v_t, mp, own, head_size):
    rows = min(BLOCK, own)
    blocks = LEN // rows
    cat = kcat.shape[1]
    return pl.pallas_call(
        functools.partial(fwd_kernel, mp, own),
        grid_spec=pltpu.PrefetchScalarGridSpec(
            num_scalar_prefetch=1,
            grid=(blocks,),
            in_specs=[
                pl.BlockSpec((1, rows, cat), lambda i, m: (head, i, 0)),
                full(kcat.shape),
                pl.BlockSpec((head_size, LEN), lambda i, m: (head, 0)),
            ],
            out_specs=[
                pl.BlockSpec((1, LEN, rows), lambda i, m: (i, 0, 0)),
                pl.BlockSpec((head_size, rows), lambda i, m: (0, i)),
                pl.BlockSpec((1, rows), lambda i, m: (0, i)),
            ]
            + [full((head_size, own))] * mp,
        ),
        out_shape=[
            jax.ShapeDtypeStruct((blocks, LEN, rows), bf16),
            jax.ShapeDtypeStruct((head_size, LEN), f32),
            jax.ShapeDtypeStruct((1, LEN), f32),
        ]
        + [jax.ShapeDtypeStruct((head_size, own), bf16)] * mp,
        compiler_params=params(),
        cost_estimate=pl.CostEstimate(
            flops=2 * LEN * LEN * (cat + head_size) * 6 // 10,
            bytes_accessed=16 << 20,
            transcendentals=LEN * LEN * 6 // 10,
        ),
        name="attend",
    )(me, qcat, kcat, v_t)


def bwd_kernel(mp, own, head, heads, score_scale, me_ref, *refs):
    g_refs = refs[:mp]
    (expon, full_t, inv, slot, kcat_t, v, shift, w_pos_t, sin_t, cos_t, norm_all) = refs[mp : mp + 11]
    out = refs[mp + 11 :]
    piece_refs = out[:mp]
    dw_out, dpos, dcb, dpb = out[mp : mp + 4]
    grad_s, dk_s, dv_s, all_s = out[mp + 4 :]
    step = pl.program_id(0)
    steps = pl.num_programs(0)
    me = me_ref[0]
    rows = inv.shape[1]
    size = full_t.shape[0]
    width = v.shape[1]
    model = w_pos_t.shape[1]
    half = model // 2
    first_row = head * size

    @pl.when(step == 0)
    def _():
        for k in range(mp):
            source = lax.rem(me - k + mp, mp)
            grad_s[:, pl.ds(pl.multiple_of(source * own, own), own)] = g_refs[k][...]
        dk_s[...] = jnp.zeros_like(dk_s)
        dv_s[...] = jnp.zeros_like(dv_s)
        dpos[...] = jnp.zeros_like(dpos)
        dcb[...] = jnp.zeros_like(dcb)
        dpb[...] = jnp.zeros_like(dpb)

    def masked_rows(part):
        if heads == 1:
            return part
        zeros = jnp.zeros((size, part.shape[1]), part.dtype)
        return jnp.concatenate([part if h == head else zeros for h in range(heads)], axis=0)

    for block in range(LEN // rows):

        @pl.when(step == block)
        def _(block=block):
            low, high = block * rows, (block + 1) * rows
            grad = grad_s[:, low:high].astype(f32) * inv[...]
            delta = jnp.sum(grad * full_t[...], axis=0, keepdims=True)
            grad = masked_rows(grad)
            grad_t = grad.astype(bf16)
            grad_n = grad.T.astype(bf16)
            exp_all = expon[0, :high]
            grad_probs = nn(v[:high], grad_t)
            grad_scores = (exp_all.astype(f32) * (grad_probs - delta)).astype(bf16)
            dv_s[:high] += nn(exp_all, grad_n)
            dk_s[:high] += nn(grad_scores, slot[0])
            joint = nn(kcat_t[first_row : first_row + size + model, :high], grad_scores)
            joint = joint * score_scale
            if head == 0:
                d_content, d_pos = joint[:size], joint[size:]
            else:
                d_content, d_pos = joint[model:], joint[:model]
            g_cos, g_sin = d_pos[:half], d_pos[half:]
            sin, cos = sin_t[...], cos_t[...]
            d_coeff = jnp.concatenate(
                [
                    (g_cos * sin - g_sin * cos).astype(bf16),
                    (g_cos * cos + g_sin * sin).astype(bf16),
                ],
                axis=0,
            )
            dpos[...] += nn(d_coeff, shift[...])
            d_shift = nn(w_pos_t[...], d_coeff)
            dcb[...] += jnp.sum(d_content, axis=1, keepdims=True)
            dpb[...] += jnp.sum(d_shift, axis=1, keepdims=True)
            all_s[:size, low:high] = (d_content + d_shift).astype(bf16)

    @pl.when(step == steps - 1)
    def _():
        mine = slice(first_row, first_row + size)
        all_s[size : 2 * size] = (dk_s[...] * (1.0 / log2_e)).T[mine].astype(bf16)
        all_s[2 * size :] = dv_s[...].T[mine].astype(bf16)
        dw_out[...] = nn(all_s[...], norm_all[...]).astype(bf16)
        for k in range(mp):
            target = lax.rem(me + k, mp)
            piece_refs[k][...] = all_s[:, pl.ds(pl.multiple_of(target * own, own), own)]


def bwd_call(
    me, head, heads, pieces, expon, full_t, inv, qcat, kcat_t, v, shift, w_pos, tables_t, norm_all, scale
):
    mp = len(pieces)
    size, own = pieces[0].shape
    blocks, _, rows = expon.shape
    width = v.shape[1]
    model = norm_all.shape[1]
    col_block = lambda n: pl.BlockSpec((n, rows), lambda i, m: (0, i))
    if width % 128 == 0:
        slot, slot_spec = qcat, pl.BlockSpec((1, rows, width), lambda i, m: (head, i, model // width))
    else:
        slot, slot_spec = qcat[:, :, model:], pl.BlockSpec((1, rows, width), lambda i, m: (head, i, 0))
    w_pos_t = w_pos[:, head * size : (head + 1) * size].T
    return pl.pallas_call(
        functools.partial(bwd_kernel, mp, own, head, heads, scale),
        grid_spec=pltpu.PrefetchScalarGridSpec(
            num_scalar_prefetch=1,
            grid=(blocks,),
            in_specs=[full((size, own))] * mp
            + [
                pl.BlockSpec((1, LEN, rows), lambda i, m: (i, 0, 0)),
                col_block(size),
                col_block(1),
                slot_spec,
                full(kcat_t.shape),
                full(v.shape),
                pl.BlockSpec((rows, width), lambda i, m: (i, 0)),
                full(w_pos_t.shape),
                col_block(model // 2),
                col_block(model // 2),
                full(norm_all.shape),
            ],
            out_specs=[full((3 * size, own))] * mp
            + [full((3 * size, model)), full((model, width)), full((size, 1)), full((size, 1))],
            scratch_shapes=[
                pltpu.VMEM((size, LEN), bf16),
                pltpu.VMEM((LEN, width), f32),
                pltpu.VMEM((LEN, width), f32),
                pltpu.VMEM((3 * size, LEN), bf16),
            ],
        ),
        out_shape=[jax.ShapeDtypeStruct((3 * size, own), bf16)] * mp
        + [
            jax.ShapeDtypeStruct((3 * size, model), bf16),
            jax.ShapeDtypeStruct((model, width), f32),
            jax.ShapeDtypeStruct((size, 1), f32),
            jax.ShapeDtypeStruct((size, 1), f32),
        ],
        compiler_params=params(),
        cost_estimate=pl.CostEstimate(
            flops=2 * LEN * LEN * (model + 4 * width) * 6 // 10, bytes_accessed=24 << 20, transcendentals=0
        ),
        name="attend_back",
    )(me, *pieces, expon, full_t, inv, slot, kcat_t, v, shift, w_pos_t, *tables_t, norm_all)


def rows_kernel(mp, heads, me_ref, *refs):
    count = heads * mp
    pieces = refs[:count]
    (ids, labels, cotangent, table, w_out, gain, bias, down_bias, logit_bias, vec, w_up, w_down, w_pred) = refs[
        count : count + 13
    ]
    out = refs[count + 13 :]
    back = out[:count]
    (block_out, grad_mid, d_up, d_down, d_pred, d_out, d_vec, d_norm, d_scalar) = out[count : count + 9]
    (att, xhat, inv, norm_mid, norm_mid_t, total, out_low, out_low_t, hidden, slope, p_hidden, p_slope, logit, g_logit) = out[
        count + 9 :
    ]
    step = pl.program_id(0)
    phase = step // mp
    c = lax.rem(step, mp)
    me = me_ref[0]
    size = pieces[0].shape[0]
    width = heads * size
    own, model = block_out.shape

    @pl.when(step == 0)
    def _():
        for h in range(heads):
            for k in range(mp):
                source = lax.rem(me - k + mp, mp)
                row = pl.multiple_of(source * width + h * size, size)
                att[pl.ds(row, size)] = pieces[h * mp + k][...]
        _, inputs = embed_rows(ids[...], table[...])
        middle = inputs + nn(att[...].astype(f32).T.astype(bf16), w_out[...])
        normed, inverse = layer_stats(middle)
        xhat[...] = normed
        inv[...] = inverse
        mid = normed * gain[...] + bias[...]
        norm_mid[...] = mid.astype(bf16)
        norm_mid_t[...] = mid.T.astype(bf16)
        total[...] = middle + down_bias[...]

    @pl.when(phase == 0)
    def _():
        pre = nn(norm_mid[...], w_up[0]) + vec[c, 0:1]
        value, grad = gelu_parts(pre)
        value = value.astype(bf16)
        hidden[c] = value
        slope[c] = grad
        total[...] += nn(value, w_down[0])

    @pl.when(step == mp - 1)
    def _():
        low = total[...].astype(bf16)
        out_low[...] = low
        block_out[...] = low
        out_low_t[...] = low.astype(f32).T.astype(bf16)
        logit[...] = jnp.zeros_like(logit)

    @pl.when(phase == 1)
    def _():
        pre = nn(out_low[...], w_pred[0]) + vec[c, 1:2]
        value, grad = gelu_parts(pre)
        value = value.astype(bf16)
        p_hidden[c] = value
        p_slope[c] = grad
        logit[...] += jnp.sum(value.astype(f32) * vec[c, 2:3], axis=1, keepdims=True)

    @pl.when(step == 2 * mp - 1)
    def _():
        label_rows = jnp.broadcast_to(labels[0].astype(f32), (128, own)).T
        label = label_rows[:, :1]
        x = logit[...] + logit_bias[...]
        fall = jnp.exp(-jnp.abs(x))
        loss = jnp.maximum(x, 0.0) + jnp.log(1.0 + fall) - label * x
        grad = jnp.where(x >= 0, 1.0, fall) / (1.0 + fall) - label
        d_scalar[0:1] = jnp.broadcast_to(jnp.sum(loss, axis=0, keepdims=True), (1, 128))
        d_scalar[1:2] = jnp.broadcast_to(jnp.sum(grad, axis=0, keepdims=True), (1, 128))
        g_logit[...] = grad.astype(bf16).astype(f32)
        total[...] = cotangent[...].astype(f32)

    @pl.when(phase == 2)
    def _():
        g = g_logit[...]
        g_pre = g * vec[c, 2:3] * p_slope[c]
        d_vec[c, 1:2] = jnp.sum(g_pre, axis=0, keepdims=True)
        d_vec[c, 2:3] = jnp.sum(g * p_hidden[c].astype(f32), axis=0, keepdims=True)
        g_low = g_pre.astype(bf16)
        d_pred[0] = nn(out_low_t[...], g_low).astype(bf16)
        total[...] += nt(g_low, w_pred[0])

    @pl.when(step == 3 * mp - 1)
    def _():
        g_out = total[...]
        d_norm[2:3] = jnp.sum(g_out, axis=0, keepdims=True)
        grad_mid[...] = g_out
        out_low[...] = g_out.astype(bf16)
        total[...] = jnp.zeros_like(total)

    @pl.when(phase == 3)
    def _():
        g_low = out_low[...]
        d_down[0] = tn(hidden[c], g_low).astype(bf16)
        g_up = nt(g_low, w_down[0]) * slope[c]
        d_vec[c, 0:1] = jnp.sum(g_up, axis=0, keepdims=True)
        g_up = g_up.astype(bf16)
        d_up[0] = nn(norm_mid_t[...], g_up).astype(bf16)
        total[...] += nt(g_up, w_up[0])

    @pl.when(step == 4 * mp - 1)
    def _():
        g_norm = total[...]
        normed = xhat[...]
        d_norm[0:1] = jnp.sum(g_norm * normed, axis=0, keepdims=True)
        d_norm[1:2] = jnp.sum(g_norm, axis=0, keepdims=True)
        g_mid = grad_mid[...] + norm_back(g_norm, normed, inv[...], gain[...])
        grad_mid[...] = g_mid
        g_low = g_mid.astype(bf16)
        d_out[...] = nn(att[...], g_low).astype(bf16)
        att[...] = nt(w_out[...], g_low).astype(bf16)
        for h in range(heads):
            for k in range(mp):
                target = lax.rem(me + k, mp)
                row = pl.multiple_of(target * width + h * size, size)
                back[h * mp + k][...] = att[pl.ds(row, size)]


def rows_call(me, pieces, heads, ids, labels, cotangent, table, w_out, gain, bias, down_bias, logit_bias, vec, weights):
    mp = vec.shape[0]
    size, own = pieces[0].shape
    model = table.shape[1]
    hid = vec.shape[2]
    total_width = mp * heads * size
    (up, up_at), (down, down_at), (pred, pred_at) = weights

    def outer(row):
        return lambda s, m: (jnp.where((s // mp == 0) | (s // mp == 3), lax.rem(s, mp), mp - 1), row, 0)

    def inner(row):
        return lambda s, m: (
            jnp.where(s // mp == 0, 0, jnp.where(s // mp == 3, mp - 1, lax.rem(s, mp))),
            row,
            0,
        )

    def last(phase):
        return lambda s, m: (
            jnp.where(s // mp < phase, 0, jnp.where(s // mp == phase, lax.rem(s, mp), mp - 1)),
            0,
            0,
        )

    outs = [jax.ShapeDtypeStruct((size, own), bf16)] * len(pieces) + [
        jax.ShapeDtypeStruct((own, model), bf16),
        jax.ShapeDtypeStruct((own, model), f32),
        jax.ShapeDtypeStruct((mp, model, hid), bf16),
        jax.ShapeDtypeStruct((mp, hid, model), bf16),
        jax.ShapeDtypeStruct((mp, model, hid), bf16),
        jax.ShapeDtypeStruct((total_width, model), bf16),
        jax.ShapeDtypeStruct((mp, 3, hid), f32),
        jax.ShapeDtypeStruct((3, model), f32),
        jax.ShapeDtypeStruct((2, 128), f32),
    ]
    out_specs = [full(o.shape) for o in outs]
    base = len(pieces)
    out_specs[base + 2] = pl.BlockSpec((1, model, hid), last(3))
    out_specs[base + 3] = pl.BlockSpec((1, hid, model), last(3))
    out_specs[base + 4] = pl.BlockSpec((1, model, hid), last(2))
    ins = [*pieces, ids]
    tail = [cotangent, table, w_out, gain, bias, down_bias, logit_bias, vec]
    return pl.pallas_call(
        functools.partial(rows_kernel, mp, heads),
        grid_spec=pltpu.PrefetchScalarGridSpec(
            num_scalar_prefetch=1,
            grid=(4 * mp,),
            in_specs=[full(a.shape) for a in ins]
            + [pl.BlockSpec((1, 1, own), lambda s, m: (m[0], 0, 0))]
            + [full(a.shape) for a in tail]
            + [
                pl.BlockSpec((1, model, hid), outer(up_at)),
                pl.BlockSpec((1, hid, model), outer(down_at)),
                pl.BlockSpec((1, model, hid), inner(pred_at)),
            ],
            out_specs=out_specs,
            scratch_shapes=[
                pltpu.VMEM((total_width, own), bf16),
                pltpu.VMEM((own, model), f32),
                pltpu.VMEM((own, 1), f32),
                pltpu.VMEM((own, model), bf16),
                pltpu.VMEM((model, own), bf16),
                pltpu.VMEM((own, model), f32),
                pltpu.VMEM((own, model), bf16),
                pltpu.VMEM((model, own), bf16),
                pltpu.VMEM((mp, own, hid), bf16),
                pltpu.VMEM((mp, own, hid), f32),
                pltpu.VMEM((mp, own, hid), bf16),
                pltpu.VMEM((mp, own, hid), f32),
                pltpu.VMEM((own, 1), f32),
                pltpu.VMEM((own, 1), f32),
            ],
        ),
        out_shape=outs,
        compiler_params=params(),
        cost_estimate=pl.CostEstimate(
            flops=18 * own * model * hid * mp, bytes_accessed=20 << 20, transcendentals=2 * own * hid * mp
        ),
        name="rows",
    )(me, *ins, labels, *tail, up, down, pred)


def tail_kernel(mp, heads, me_ref, *refs):
    count = heads * mp
    pieces = refs[:count]
    w_joint, ids, table, gain, grad_mid, grad_in, d_embed, d_norm, parts = refs[count:]
    me = me_ref[0]
    third = pieces[0].shape[0]
    width = heads * third
    for h in range(heads):
        for k in range(mp):
            source = lax.rem(me - k + mp, mp)
            row = pl.multiple_of(source * width + h * third, third)
            parts[pl.ds(row, third)] = pieces[h * mp + k][...]
    g_norm = tn(parts[...], w_joint[...])
    one_hot_t, inputs = embed_rows(ids[...], table[...])
    normed, inverse = layer_stats(inputs)
    d_norm[0:1] = jnp.sum(g_norm * normed, axis=0, keepdims=True)
    d_norm[1:2] = jnp.sum(g_norm, axis=0, keepdims=True)
    g_in = grad_mid[...] + norm_back(g_norm, normed, inverse, gain[...])
    first = g_in.astype(bf16)
    grad_in[...] = first
    rest = g_in - first.astype(f32)
    second = rest.astype(bf16)
    third_part = (rest - second.astype(f32)).astype(bf16)
    hot = one_hot_t.astype(bf16)
    d_embed[...] = nn(hot, first) + nn(hot, second) + nn(hot, third_part)


def tail_call(me, pieces, heads, w_joint, ids, table, gain, grad_mid):
    mp = len(pieces) // heads
    own, model = grad_mid.shape
    outs = [
        jax.ShapeDtypeStruct((own, model), bf16),
        jax.ShapeDtypeStruct(table.shape, f32),
        jax.ShapeDtypeStruct((2, model), f32),
    ]
    ins = [*pieces, w_joint, ids, table, gain, grad_mid]
    return pl.pallas_call(
        functools.partial(tail_kernel, mp, heads),
        grid_spec=pltpu.PrefetchScalarGridSpec(
            num_scalar_prefetch=1,
            grid=(1,),
            in_specs=[full(a.shape) for a in ins],
            out_specs=[full(o.shape) for o in outs],
            scratch_shapes=[pltpu.VMEM(w_joint.shape, bf16) if w_joint.shape[1] == own else pltpu.VMEM((w_joint.shape[0], own), bf16)],
        ),
        out_shape=outs,
        compiler_params=params(),
        cost_estimate=pl.CostEstimate(flops=4 * own * model * model, bytes_accessed=6 << 20, transcendentals=0),
        name="tail",
    )(me, *ins)


def shift_pairs(count, k):
    return [(s, (s + k) % count) for s in range(count)]


def exchange(parts, axis, count):
    return [parts[0]] + [
        lax.ppermute(parts[k], axis, shift_pairs(count, k)) for k in range(1, count)
    ]


def swap(value, axis, count, bit):
    return lax.ppermute(value, axis, [(s, s ^ bit) for s in range(count)])


def sum_all(value, dp, mp):
    rows = value.shape[0]
    me_dp, me_mp = lax.axis_index("dp"), lax.axis_index("mp")
    bits = []
    bit = 1
    while bit < dp:
        bits.append(bit)
        bit *= 2
    current = value
    for bit in bits:
        half = current.shape[0] // 2
        mine = (me_dp // bit) % 2
        kept = lax.dynamic_slice_in_dim(current, mine * half, half, 0)
        sent = lax.dynamic_slice_in_dim(current, (1 - mine) * half, half, 0).astype(bf16)
        current = kept + swap(sent, "dp", dp, bit).astype(f32)
    piece = current.shape[0] // mp
    sent = [
        lax.dynamic_slice_in_dim(current, ((me_mp + k) % mp) * piece, piece, 0) for k in range(mp)
    ]
    got = exchange([sent[0]] + [s.astype(bf16) for s in sent[1:]], "mp", mp)
    low = sum(g.astype(f32) for g in got).astype(bf16)
    back = exchange([low] * mp, "mp", mp)
    current = jnp.zeros((piece * mp, value.shape[1]), bf16)
    for k in range(mp):
        current = lax.dynamic_update_slice_in_dim(
            current, back[k], ((me_mp - k) % mp) * piece, 0
        )
    for bit in reversed(bits):
        other = swap(current, "dp", dp, bit)
        mine = (me_dp // bit) % 2
        current = jnp.where(
            mine == 0,
            jnp.concatenate([current, other], axis=0),
            jnp.concatenate([other, current], axis=0),
        )
    return current.astype(f32)


def per_device(
    byte_ids,
    embed_table,
    boundary_labels,
    out_cotangent,
    norm_one_gain,
    norm_one_bias,
    w_query,
    w_key,
    w_value,
    w_position,
    content_bias,
    position_bias,
    w_out,
    norm_two_gain,
    norm_two_bias,
    w_up,
    up_bias,
    w_down,
    down_bias,
    w_pred,
    pred_bias,
    w_logit,
    logit_bias,
):
    dp, mp = lax.axis_size("dp"), lax.axis_size("mp")
    me_dp, me_mp = lax.axis_index("dp"), lax.axis_index("mp")
    own = byte_ids.shape[0]
    assert boundary_labels.shape[0] == LEN and own * mp == LEN
    model = embed_table.shape[1]
    heads, size = content_bias.shape
    width = heads * size
    hid = w_up.shape[1]
    scale = 1.0 / math.sqrt(size)
    me = me_mp.astype(jnp.int32).reshape(1)
    row = lambda v: v.astype(f32).reshape(1, -1)

    joint_t = (
        jnp.stack([w_query.T, w_key.T, w_value.T])
        .reshape(3, heads, size, model)
        .transpose(1, 0, 2, 3)
        .reshape(3 * width, model)
    )
    flat = jnp.concatenate([up_bias, pred_bias, w_logit]).reshape(-1)
    rows_used = 3 * hid + 4 * width
    unit = dp * 16
    total_rows = -(-(rows_used + -(-flat.shape[0] // model)) // unit) * unit
    flat = jnp.pad(flat, (0, (total_rows - rows_used) * model - flat.shape[0]))
    pack = jnp.concatenate(
        [
            w_up.reshape(hid, model),
            w_down,
            w_pred.reshape(hid, model),
            w_out,
            joint_t,
            flat.reshape(-1, model),
        ],
        axis=0,
    )
    share = total_rows // dp
    pack = lax.dynamic_slice_in_dim(pack, me_dp * share, share, 0)
    whole = lax.all_gather(pack, ("mp", "dp"), axis=0, tiled=True).reshape(mp, total_rows, model)

    def weight(index, shape):
        if shape == (hid, model):
            return whole, index
        return whole[:, index * hid : (index + 1) * hid].reshape(mp, *shape), 0

    weights = (weight(0, (model, hid)), weight(1, (hid, model)), weight(2, (model, hid)))
    out_whole = whole[:, 3 * hid : 3 * hid + width].reshape(mp * width, model)
    joint_whole = whole[:, 3 * hid + width : rows_used].reshape(mp * 3 * width, model)
    vec = whole[:, rows_used:].reshape(mp, -1)[:, : 3 * hid].reshape(mp, 3, hid).astype(f32)

    sin_np, cos_np = feature_tables(model)
    feature = np.concatenate([cos_np, sin_np], axis=1).astype(jnp.bfloat16)
    tables = (
        jnp.asarray(feature),
        jnp.asarray(np.ascontiguousarray(feature.T)),
        jnp.asarray(sin_np),
        jnp.asarray(cos_np),
    )
    tables_t = (
        jnp.asarray(np.ascontiguousarray(sin_np.T)),
        jnp.asarray(np.ascontiguousarray(cos_np.T)),
    )

    ids_own = byte_ids.reshape(1, own)
    id_parts = exchange([ids_own] * mp, "mp", mp)
    w_joint = jnp.concatenate([w_query, w_key, w_value], axis=1)
    norm_all, qcat, kcat, kcat_t, v, v_t, shift = pre_call(
        me,
        id_parts,
        embed_table,
        row(norm_one_gain),
        row(norm_one_bias),
        w_joint,
        w_position,
        row(content_bias),
        row(position_bias),
        tables,
        heads,
        scale,
    )
    saved, sent = [], []
    for h in range(heads):
        expon, full_t, inv, *parts = fwd_call(me, h, qcat, kcat, v_t, mp, own, size)
        saved.append((expon, full_t, inv))
        sent += exchange(parts, "mp", mp)

    result = rows_call(
        me,
        sent,
        heads,
        ids_own,
        boundary_labels.reshape(mp, 1, own),
        out_cotangent,
        embed_table,
        out_whole,
        row(norm_two_gain),
        row(norm_two_bias),
        row(down_bias),
        row(logit_bias),
        vec,
        weights,
    )
    back = result[: heads * mp]
    block_out, grad_mid, d_up, d_down, d_pred, d_out, d_vec, d_norm_two, d_scalar = result[heads * mp :]

    d_flat = jnp.pad(
        d_vec.reshape(mp, 3 * hid).astype(bf16),
        ((0, 0), (0, (total_rows - rows_used) * model - 3 * hid)),
    ).reshape(mp, -1, model)
    grads = jnp.concatenate(
        [
            d_up.reshape(mp, hid, model),
            d_down,
            d_pred.reshape(mp, hid, model),
            d_out.reshape(mp, width, model),
            d_flat,
        ],
        axis=1,
    )
    used = grads.shape[1]
    extra = -used % (dp * 8)
    grads = jnp.pad(grads, ((0, 0), (0, extra), (0, 0)))
    grads = grads.reshape(mp, dp, (used + extra) // dp, model)
    grads = lax.psum_scatter(grads, "dp", scatter_dimension=1, tiled=True)
    grads = lax.psum_scatter(grads, "mp", scatter_dimension=0, tiled=True)
    grads = lax.all_gather(grads.reshape(-1, model), "dp", axis=0, tiled=True).astype(f32)

    arrived, d_joint, d_pos, d_cb, d_pb = [], [], 0.0, [], []
    for h in range(heads):
        pieces = exchange(back[h * mp : (h + 1) * mp], "mp", mp)
        parts = bwd_call(
            me,
            h,
            heads,
            pieces,
            *saved[h],
            qcat,
            kcat_t,
            v,
            shift,
            w_position,
            tables_t,
            norm_all,
            scale,
        )
        arrived += exchange(parts[:mp], "mp", mp)
        dw, dp_, dc, db = parts[mp:]
        d_joint.append(dw)
        lane = jnp.arange(width)[None, :]
        d_pos = d_pos + jnp.where((lane >= h * size) & (lane < (h + 1) * size), dp_, 0.0)
        d_cb.append(dc)
        d_pb.append(db)
    grad_input, d_embed, d_norm_one = tail_call(
        me, arrived, heads, joint_whole, ids_own, embed_table, row(norm_one_gain), grad_mid
    )

    bias_rows = jnp.concatenate(
        [jnp.concatenate(d_cb, axis=0), jnp.concatenate(d_pb, axis=0)], axis=0
    ).reshape(-1)
    bias_rows = jnp.pad(bias_rows, (0, 8 * model - bias_rows.shape[0])).reshape(8, model)
    by_seq = jnp.concatenate(
        [*d_joint, d_pos.reshape(-1, model).astype(bf16), bias_rows.astype(bf16)], axis=0
    )
    by_seq = lax.psum(by_seq, "dp").astype(f32)
    joint = by_seq[: 3 * width].reshape(heads, 3, size, model).transpose(1, 0, 2, 3)
    joint = joint.reshape(3, width, model).transpose(0, 2, 1)
    sum_pos = by_seq[3 * width : 4 * width].reshape(model, width)
    sum_bias = by_seq[4 * width :].reshape(-1)
    sum_cb = sum_bias[:width].reshape(heads, size)
    sum_pb = sum_bias[width : 2 * width].reshape(heads, size)

    scalars = lax.psum(d_scalar, ("dp", "mp"))
    vocab = embed_table.shape[0]
    small = jnp.concatenate([d_norm_one, d_norm_two], axis=0)
    pad_rows = -(vocab + 5) % (dp * mp * 8)
    sums = sum_all(
        jnp.concatenate([d_embed, small, jnp.zeros((pad_rows, model), f32)], axis=0), dp, mp
    )
    vec_sum = grads[3 * hid + width : used].reshape(-1)
    return (
        block_out,
        scalars[0, :1] / (LEN * dp),
        grad_input,
        sums[:vocab],
        sums[vocab],
        sums[vocab + 1],
        joint[0],
        joint[1],
        joint[2],
        sum_pos,
        sum_cb,
        sum_pb,
        grads[3 * hid : 3 * hid + width],
        sums[vocab + 2],
        sums[vocab + 3],
        grads[:hid].reshape(model, hid),
        vec_sum[:hid],
        grads[hid : 2 * hid],
        sums[vocab + 4],
        grads[2 * hid : 3 * hid].reshape(model, hid),
        vec_sum[hid : 2 * hid],
        vec_sum[2 * hid : 3 * hid],
        scalars[1, :1],
    )


def solution(mesh):
    by_rows = P(("dp", "mp"), None)
    columns = P(None, "mp")
    shard = P("mp", None)
    placed = (
        P(("dp", "mp")),
        P(),
        P("dp"),
        by_rows,
        P(),
        P(),
        columns,
        columns,
        columns,
        columns,
        shard,
        shard,
        shard,
        P(),
        P(),
        columns,
        P("mp"),
        shard,
        P(),
        columns,
        P("mp"),
        P("mp"),
        P(),
    )
    results = (
        by_rows,
        P(),
        by_rows,
        P(),
        P(),
        P(),
        columns,
        columns,
        columns,
        columns,
        shard,
        shard,
        shard,
        P(),
        P(),
        columns,
        P("mp"),
        shard,
        P(),
        columns,
        P("mp"),
        P("mp"),
        P(),
    )
    return jax.shard_map(
        per_device, mesh=mesh, in_specs=placed, out_specs=results, check_vma=False
    )
```

```python
import functools
import math

import jax
import jax.numpy as jnp
import numpy as np
from jax import lax
from jax.experimental import pallas as pl
from jax.experimental.pallas import tpu as pltpu
from jax.sharding import PartitionSpec as P

LEN = 2048
BLOCK = 256
VMEM_BYTES = 56 * 1024 * 1024
SMALL_VMEM_BYTES = 20 * 1024 * 1024

bf16 = jnp.bfloat16
f32 = jnp.float32
norm_eps = 1e-05
density_scale = 1.0 / math.sqrt(2.0 * math.pi)
log2_e = math.log2(math.e)


def nn(first, second):
    return jnp.dot(first, second, preferred_element_type=f32)


def nt(first, second):
    return lax.dot_general(
        first, second, (((1,), (1,)), ((), ())), preferred_element_type=f32
    )


def tn(first, second):
    return lax.dot_general(
        first, second, (((0,), (0,)), ((), ())), preferred_element_type=f32
    )


def layer_stats(values):
    centered = values - jnp.mean(values, axis=-1, keepdims=True)
    inverse = lax.rsqrt(jnp.mean(centered * centered, axis=-1, keepdims=True) + norm_eps)
    return centered * inverse, inverse


def norm_back(grad_normed, normed, inverse, gain_row):
    scaled = grad_normed * gain_row
    first_mean = jnp.mean(scaled, axis=-1, keepdims=True)
    second_mean = jnp.mean(scaled * normed, axis=-1, keepdims=True)
    return inverse * (scaled - first_mean - normed * second_mean)


def gelu_parts(values):
    size = jnp.abs(values)
    fall = jnp.exp(-0.5 * values * values)
    t = 1.0 / (1.0 + (0.3275911 / math.sqrt(2.0)) * size)
    poly = 1.061405429 * t - 1.453152027
    poly = poly * t + 1.421413741
    poly = poly * t - 0.284496736
    poly = poly * t + 0.254829592
    tail = 0.5 * poly * t * fall
    phi = jnp.where(values >= 0, 1.0 - tail, tail)
    return values * phi, phi + values * fall * density_scale


def feature_tables(model_width):
    half = model_width // 2
    frequency = np.exp(
        np.arange(half, dtype=np.float64) * (-2.0 * math.log(10000.0) / model_width)
    )
    angles = np.arange(LEN, dtype=np.float64)[:, None] * frequency[None, :]
    return np.sin(angles).astype(np.float32), np.cos(angles).astype(np.float32)


def embed_rows(ids_row, table):
    vocab = table.shape[0]
    places = lax.broadcasted_iota(jnp.int32, (vocab, ids_row.shape[1]), 0)
    one_hot_t = (places == ids_row.astype(jnp.int32)).astype(f32)
    rows = nn(one_hot_t.T.astype(bf16), table)
    return one_hot_t, rows


def full(shape):
    return pl.BlockSpec(shape, lambda *_: (0,) * len(shape))


def params():
    return pltpu.CompilerParams(vmem_limit_bytes=VMEM_BYTES)


def prep_kernel(dp, me_ref, *refs):
    (ids, up_bias, pred_bias, w_logit, gain1, bias1, gain2, bias2, down_bias, cb, pb, logit_bias, labels) = refs[:13]
    w_query, w_key, w_value, w_pos = refs[13:17]
    weights = refs[17:21] if dp else ()
    out = refs[17 + len(weights) :]
    head_rows, vecs, biases, label_rows, logit_b, w_joint, w_pos_t, joint_t = out[:8]
    copies = []
    width = w_query.shape[1]
    for place, ref in enumerate((w_query, w_key, w_value)):
        w_joint[:, place * width : (place + 1) * width] = ref[...]
        joint_t[place * width : (place + 1) * width] = ref[...].astype(f32).T.astype(bf16)
    if dp:
        shares, sems = out[8:]
        row = 0
        for place, ref in enumerate(weights):
            rows = ref.shape[0] // dp
            start = pl.multiple_of(me_ref[1] * rows, rows)
            copy = pltpu.make_async_copy(
                ref.at[pl.ds(start, rows)], shares.at[pl.ds(row, rows)], sems.at[place]
            )
            copy.start()
            copies.append(copy)
            row += rows
        rows = joint_t.shape[0] // dp
        start = pl.multiple_of(me_ref[1] * rows, rows)
        shares[row : row + rows] = joint_t[pl.ds(start, rows)]
    own = ids.shape[0]
    row_of = lambda ref: ref[...].astype(f32).reshape(1, -1)
    head_rows[...] = jnp.zeros_like(head_rows)
    for place, ref in enumerate((ids, up_bias, pred_bias, w_logit)):
        head_rows[place : place + 1] = row_of(ref).astype(bf16)
    vecs[...] = jnp.zeros_like(vecs)
    for place, ref in enumerate((gain1, bias1, gain2, bias2, down_bias)):
        vecs[place : place + 1] = row_of(ref)
    heads = cb.shape[0]
    for place, ref in enumerate((cb, pb)):
        rows = [ref[h : h + 1].astype(f32) for h in range(heads)]
        biases[place : place + 1] = jnp.concatenate(rows, axis=1) if heads > 1 else rows[0]
    for z in range(label_rows.shape[0]):
        label_rows[z] = labels[z * own : (z + 1) * own].astype(f32).reshape(1, own)
    logit_b[...] = logit_bias[...].astype(f32).reshape(1, 1)
    w_pos_t[...] = w_pos[...].astype(f32).T.astype(bf16)
    for copy in copies:
        copy.wait()


def prep_call(me, ins, weights, mp, dp):
    own, vec = ins[0].shape[0], ins[4].shape[0]
    width = ins[13].shape[1]
    outs = [
        jax.ShapeDtypeStruct((16, own), bf16),
        jax.ShapeDtypeStruct((8, vec), f32),
        jax.ShapeDtypeStruct((2, width), f32),
        jax.ShapeDtypeStruct((mp, 1, own), f32),
        jax.ShapeDtypeStruct((1, 1), f32),
        jax.ShapeDtypeStruct((vec, 3 * width), bf16),
        jax.ShapeDtypeStruct((width, vec), bf16),
        jax.ShapeDtypeStruct((3 * width, vec), bf16),
    ]
    scratch = []
    if dp:
        rows = (sum(w.shape[0] for w in weights) + 3 * width) // dp
        outs.append(jax.ShapeDtypeStruct((rows, vec), bf16))
        scratch = [pltpu.SemaphoreType.DMA((len(weights),))]
        ins = [*ins, *weights]
    return pl.pallas_call(
        functools.partial(prep_kernel, dp),
        grid_spec=pltpu.PrefetchScalarGridSpec(
            num_scalar_prefetch=1,
            grid=(1,),
            in_specs=[full(a.shape) for a in ins[:17]]
            + [pl.BlockSpec(memory_space=pl.ANY)] * (len(ins) - 17),
            out_specs=[full(o.shape) for o in outs],
            scratch_shapes=scratch,
        ),
        out_shape=outs,
        compiler_params=params(),
        name="prepare",
    )(me, *ins)


def pre_kernel(mp, heads, score_scale, me_ref, *refs):
    id_refs = refs[:mp]
    (table, vecs, w_joint, w_pos, biases, feature, feature_t, sines, cosines) = refs[mp : mp + 9]
    norm_out, qcat, kcat, kcat_t, v_out, v_t, shift_out, ids_s = refs[mp + 9 :]
    step = pl.program_id(0)
    me = me_ref[0]
    own = id_refs[0].shape[1]

    @pl.when(step == 0)
    def _():
        for k in range(mp):
            source = lax.rem(me - k + mp, mp)
            ids_s[:, pl.ds(pl.multiple_of(source * own, own), own)] = id_refs[k][0:1].astype(f32)

    rows = norm_out.shape[0]
    ids = ids_s[:, pl.ds(pl.multiple_of(step * rows, rows), rows)]
    _, inputs = embed_rows(ids, table[...])
    normed, _ = layer_stats(inputs)
    norm_in = (normed * vecs[0:1] + vecs[1:2]).astype(bf16)
    norm_out[...] = norm_in
    joint = nn(norm_in, w_joint[...])
    width = v_out.shape[1]
    head_size = width // heads
    raw = joint[:, :width]
    keys = joint[:, width : 2 * width].astype(bf16)
    values = joint[:, 2 * width :].astype(bf16)
    v_out[...] = values
    v_t[...] = values.astype(f32).T.astype(bf16)
    model = feature.shape[1]
    half = model // 2
    kcat[:, :model] = feature[...]
    kcat[:, model:] = keys
    keys_t = keys.astype(f32).T.astype(bf16)
    kcat_t[:head_size] = keys_t[:head_size]
    kcat_t[head_size : head_size + model] = feature_t[...]
    if heads > 1:
        kcat_t[head_size + model :] = keys_t[head_size:]
    shift = (raw + biases[1:2]).astype(bf16)
    shift_out[...] = shift
    fold = score_scale * log2_e
    content = (raw + biases[0:1]) * fold
    lane = lax.broadcasted_iota(jnp.int32, content.shape, 1)
    sin, cos = sines[...], cosines[...]
    for h in range(heads):
        low, high = h * head_size, (h + 1) * head_size
        coeffs = nt(shift[:, low:high], w_pos[:, low:high])
        c_sin, c_cos = coeffs[:, :half] * fold, coeffs[:, half:] * fold
        qcat[h, :, :half] = (c_sin * sin + c_cos * cos).astype(bf16)
        qcat[h, :, half:model] = (c_cos * sin - c_sin * cos).astype(bf16)
        mine = (lane >= low) & (lane < high)
        qcat[h, :, model:] = jnp.where(mine, content, 0.0).astype(bf16)


def pre_call(me, id_parts, table, vecs, w_joint, w_pos, biases, tables, heads, scale):
    mp = len(id_parts)
    own = id_parts[0].shape[1]
    model = table.shape[1]
    width = w_pos.shape[1]
    rows = BLOCK
    feature, feature_t, sines, cosines = tables
    cat = model + width
    row_block = lambda n: pl.BlockSpec((rows, n), lambda i, m: (i, 0))
    col_block = lambda n: pl.BlockSpec((n, rows), lambda i, m: (0, i))
    ins = [*id_parts, table, vecs, w_joint, w_pos, biases]
    return pl.pallas_call(
        functools.partial(pre_kernel, mp, heads, scale),
        grid_spec=pltpu.PrefetchScalarGridSpec(
            num_scalar_prefetch=1,
            grid=(LEN // rows,),
            in_specs=[full(a.shape) for a in ins]
            + [row_block(model), col_block(model), row_block(model // 2), row_block(model // 2)],
            out_specs=[
                row_block(model),
                pl.BlockSpec((heads, rows, cat), lambda i, m: (0, i, 0)),
                row_block(cat),
                col_block(cat),
                row_block(width),
                col_block(width),
                row_block(width),
            ],
            scratch_shapes=[pltpu.VMEM((1, mp * own), f32)],
        ),
        out_shape=[
            jax.ShapeDtypeStruct((LEN, model), bf16),
            jax.ShapeDtypeStruct((heads, LEN, cat), bf16),
            jax.ShapeDtypeStruct((LEN, cat), bf16),
            jax.ShapeDtypeStruct((cat, LEN), bf16),
            jax.ShapeDtypeStruct((LEN, width), bf16),
            jax.ShapeDtypeStruct((width, LEN), bf16),
            jax.ShapeDtypeStruct((LEN, width), bf16),
        ],
        compiler_params=params(),
        cost_estimate=pl.CostEstimate(
            flops=2 * LEN * model * (table.shape[0] + 4 * width), bytes_accessed=24 << 20, transcendentals=0
        ),
        name="project",
    )(me, *ins, feature, feature_t, sines, cosines)


def fwd_kernel(mp, own, me_ref, qcat, kcat, v_t, expon_out, full_t, inv_out, *piece_refs):
    step = pl.program_id(0)
    me = me_ref[0]
    rows = qcat.shape[1]
    for block in range(LEN // rows):

        @pl.when(step == block)
        def _(block=block):
            low, high = block * rows, (block + 1) * rows
            queries = qcat[0]
            last = nt(kcat[low:high], queries)
            key_place = lax.broadcasted_iota(jnp.int32, last.shape, 0)
            query_place = lax.broadcasted_iota(jnp.int32, last.shape, 1)
            last = jnp.where(key_place <= query_place, last, -1e30)
            top = jnp.max(last, axis=0, keepdims=True)
            if block:
                first = nt(kcat[:low], queries)
                top = jnp.maximum(top, jnp.max(first, axis=0, keepdims=True))
            e_last = jnp.exp2(last - top)
            total = jnp.sum(e_last, axis=0, keepdims=True)
            e_last = e_last.astype(bf16)
            expon_out[0, low:high] = e_last
            mixed = nn(v_t[:, low:high], e_last)
            if block:
                e_first = jnp.exp2(first - top)
                total = total + jnp.sum(e_first, axis=0, keepdims=True)
                e_first = e_first.astype(bf16)
                expon_out[0, :low] = e_first
                mixed = mixed + nn(v_t[:, :low], e_first)
            inverse = 1.0 / total
            inv_out[...] = inverse
            mixed = mixed * inverse
            full_t[...] = mixed
            relative = lax.rem(low // own - me + mp, mp)
            start = low % own
            for k in range(mp):

                @pl.when(relative == k)
                def _(k=k):
                    piece_refs[k][:, start : start + rows] = mixed.astype(bf16)


def fwd_call(me, head, qcat, kcat, v_t, mp, own, head_size):
    rows = min(BLOCK, own)
    blocks = LEN // rows
    cat = kcat.shape[1]
    return pl.pallas_call(
        functools.partial(fwd_kernel, mp, own),
        grid_spec=pltpu.PrefetchScalarGridSpec(
            num_scalar_prefetch=1,
            grid=(blocks,),
            in_specs=[
                pl.BlockSpec((1, rows, cat), lambda i, m: (head, i, 0)),
                full(kcat.shape),
                pl.BlockSpec((head_size, LEN), lambda i, m: (head, 0)),
            ],
            out_specs=[
                pl.BlockSpec((1, LEN, rows), lambda i, m: (i, 0, 0)),
                pl.BlockSpec((head_size, rows), lambda i, m: (0, i)),
                pl.BlockSpec((1, rows), lambda i, m: (0, i)),
            ]
            + [full((head_size, own))] * mp,
        ),
        out_shape=[
            jax.ShapeDtypeStruct((blocks, LEN, rows), bf16),
            jax.ShapeDtypeStruct((head_size, LEN), f32),
            jax.ShapeDtypeStruct((1, LEN), f32),
        ]
        + [jax.ShapeDtypeStruct((head_size, own), bf16)] * mp,
        compiler_params=params(),
        cost_estimate=pl.CostEstimate(
            flops=2 * LEN * LEN * (cat + head_size) * 6 // 10,
            bytes_accessed=16 << 20,
            transcendentals=LEN * LEN * 6 // 10,
        ),
        name="attend",
    )(me, qcat, kcat, v_t)


def bwd_kernel(mp, own, head, heads, score_scale, me_ref, *refs):
    g_refs = refs[:mp]
    (expon, full_t, inv, slot, kcat_t, v, shift, w_pos_t, sin_t, cos_t, norm_all) = refs[mp : mp + 11]
    out = refs[mp + 11 :]
    piece_refs = out[:mp]
    dw_out, dpos, d_bias = out[mp : mp + 3]
    grad_s, dk_s, dv_s, all_s, db_s = out[mp + 3 :]
    step = pl.program_id(0)
    steps = pl.num_programs(0)
    me = me_ref[0]
    rows = inv.shape[1]
    size = full_t.shape[0]
    width = v.shape[1]
    model = w_pos_t.shape[1]
    half = model // 2
    first_row = head * size

    @pl.when(step == 0)
    def _():
        for k in range(mp):
            source = lax.rem(me - k + mp, mp)
            grad_s[:, pl.ds(pl.multiple_of(source * own, own), own)] = g_refs[k][...]
        dk_s[...] = jnp.zeros_like(dk_s)
        dv_s[...] = jnp.zeros_like(dv_s)
        dpos[...] = jnp.zeros_like(dpos)
        db_s[...] = jnp.zeros_like(db_s)

    def masked_rows(part):
        if heads == 1:
            return part
        zeros = jnp.zeros((size, part.shape[1]), part.dtype)
        return jnp.concatenate([part if h == head else zeros for h in range(heads)], axis=0)

    for block in range(LEN // rows):

        @pl.when(step == block)
        def _(block=block):
            low, high = block * rows, (block + 1) * rows
            grad = grad_s[:, low:high].astype(f32) * inv[...]
            delta = jnp.sum(grad * full_t[...], axis=0, keepdims=True)
            grad = masked_rows(grad)
            grad_t = grad.astype(bf16)
            grad_n = grad.T.astype(bf16)
            exp_all = expon[0, :high]
            grad_probs = nn(v[:high], grad_t)
            grad_scores = (exp_all.astype(f32) * (grad_probs - delta)).astype(bf16)
            dv_s[:high] += nn(exp_all, grad_n)
            dk_s[:high] += nn(grad_scores, slot[0])
            joint = nn(kcat_t[first_row : first_row + size + model, :high], grad_scores)
            joint = joint * score_scale
            if head == 0:
                d_content, d_pos = joint[:size], joint[size:]
            else:
                d_content, d_pos = joint[model:], joint[:model]
            g_cos, g_sin = d_pos[:half], d_pos[half:]
            sin, cos = sin_t[...], cos_t[...]
            d_coeff = jnp.concatenate(
                [
                    (g_cos * sin - g_sin * cos).astype(bf16),
                    (g_cos * cos + g_sin * sin).astype(bf16),
                ],
                axis=0,
            )
            dpos[...] += nn(d_coeff, shift[...])
            d_shift = nn(w_pos_t[...], d_coeff)
            db_s[:, :1] += jnp.sum(d_content, axis=1, keepdims=True)
            db_s[:, 1:2] += jnp.sum(d_shift, axis=1, keepdims=True)
            all_s[:size, low:high] = (d_content + d_shift).astype(bf16)

    @pl.when(step == steps - 1)
    def _():
        mine = slice(first_row, first_row + size)
        all_s[size : 2 * size] = (dk_s[...] * (1.0 / log2_e)).T[mine].astype(bf16)
        all_s[2 * size :] = dv_s[...].T[mine].astype(bf16)
        dw_out[...] = nn(all_s[...], norm_all[...]).astype(bf16)
        both = jnp.concatenate([db_s[:, :1], db_s[:, 1:2]], axis=0)
        d_bias[...] = jnp.broadcast_to(both, (2 * size, 128)).T[:8]
        for k in range(mp):
            target = lax.rem(me + k, mp)
            piece_refs[k][...] = all_s[:, pl.ds(pl.multiple_of(target * own, own), own)]


def bwd_call(
    me, head, heads, pieces, expon, full_t, inv, qcat, kcat_t, v, shift, w_pos_t, tables_t, norm_all, scale
):
    mp = len(pieces)
    size, own = pieces[0].shape
    blocks, _, rows = expon.shape
    width = v.shape[1]
    model = norm_all.shape[1]
    col_block = lambda n: pl.BlockSpec((n, rows), lambda i, m: (0, i))
    if width % 128 == 0:
        slot, slot_spec = qcat, pl.BlockSpec((1, rows, width), lambda i, m: (head, i, model // width))
    else:
        slot, slot_spec = qcat[:, :, model:], pl.BlockSpec((1, rows, width), lambda i, m: (head, i, 0))
    return pl.pallas_call(
        functools.partial(bwd_kernel, mp, own, head, heads, scale),
        grid_spec=pltpu.PrefetchScalarGridSpec(
            num_scalar_prefetch=1,
            grid=(blocks,),
            in_specs=[full((size, own))] * mp
            + [
                pl.BlockSpec((1, LEN, rows), lambda i, m: (i, 0, 0)),
                col_block(size),
                col_block(1),
                slot_spec,
                full(kcat_t.shape),
                full(v.shape),
                pl.BlockSpec((rows, width), lambda i, m: (i, 0)),
                pl.BlockSpec((size, model), lambda i, m: (head, 0)),
                col_block(model // 2),
                col_block(model // 2),
                full(norm_all.shape),
            ],
            out_specs=[full((3 * size, own))] * mp
            + [full((3 * size, model)), full((model, width)), full((8, 2 * size))],
            scratch_shapes=[
                pltpu.VMEM((size, LEN), bf16),
                pltpu.VMEM((LEN, width), f32),
                pltpu.VMEM((LEN, width), f32),
                pltpu.VMEM((3 * size, LEN), bf16),
                pltpu.VMEM((size, 128), f32),
            ],
        ),
        out_shape=[jax.ShapeDtypeStruct((3 * size, own), bf16)] * mp
        + [
            jax.ShapeDtypeStruct((3 * size, model), bf16),
            jax.ShapeDtypeStruct((model, width), f32),
            jax.ShapeDtypeStruct((8, 2 * size), f32),
        ],
        compiler_params=params(),
        cost_estimate=pl.CostEstimate(
            flops=2 * LEN * LEN * (model + 4 * width) * 6 // 10, bytes_accessed=24 << 20, transcendentals=0
        ),
        name="attend_back",
    )(me, *pieces, expon, full_t, inv, slot, kcat_t, v, shift, w_pos_t, *tables_t, norm_all)


def rows_kernel(mp, heads, dp, me_ref, *refs):
    count = heads * mp
    pieces, id_parts = refs[:count], refs[count : count + mp]
    refs = refs[count + mp :]
    (labels, cotangent, table, vecs, logit_bias, own_up, own_down, own_pred, own_out) = refs[:9]
    w_up, w_down, w_pred, w_out = refs[9:13]
    out = refs[13:]
    back = out[:count]
    block_out, grad_mid, d_vec, d_norm, d_scalar = out[count : count + 5]
    if dp:
        d_all, stage, stage_out, sems = out[count + 5], out[-3], out[-2], out[-1]
        out = out[count + 6 : -3]
    else:
        d_up, d_down, d_pred, d_out = out[count + 5 : count + 9]
        out = out[count + 9 :]
    (att, xhat, inv, norm_mid, norm_mid_t, total, out_low, out_low_t, hidden, slope, p_hidden, p_slope, logit, g_logit, vec) = out
    gain, bias, down_bias = vecs[2:3], vecs[3:4], vecs[4:5]
    step = pl.program_id(0)
    phase = step // mp
    c = lax.rem(step, mp)
    me = me_ref[0]
    place = lax.rem(me - c + mp, mp)
    size = pieces[0].shape[0]
    width = heads * size
    own, model = block_out.shape
    hid = own_up.shape[1]
    kinds = ("up", "down", "pred")

    def matrix(ref):
        return ref[...].reshape(-1, ref.shape[-1])

    def out_rows(k):
        if k == 0:
            return own_out[...]
        part = w_out[:, k - 1] if dp else w_out[k - 1]
        return part.reshape(width, model)

    def chunk_step(wanted, body):
        @pl.when((phase == wanted) & (c == 0))
        def _():
            body(*(ref[...] for ref in (own_up, own_down, own_pred)))

        @pl.when((phase == wanted) & (c > 0))
        def _():
            body(*(matrix(ref) for ref in (w_up, w_down, w_pred)))

    def copy_out(kind, chunk):
        index = kinds.index(kind)
        rows = stage.shape[3]
        target = d_all.at[:, lax.rem(me - chunk + mp, mp), pl.ds(index * rows, rows)]
        return pltpu.make_async_copy(stage.at[index, chunk], target, sems.at[index, chunk])

    def store(kind, value):
        if not dp:
            {"up": d_up, "down": d_down, "pred": d_pred}[kind][0] = value.astype(bf16)
            return
        stage[kinds.index(kind), c] = value.astype(bf16).reshape(stage.shape[2:])
        copy_out(kind, c).start()

    @pl.when(step == 0)
    def _():
        for k in range(mp):
            vec[k] = id_parts[k][1:4].astype(f32)
            for h in range(heads):
                row = k * width + h * size
                att[row : row + size] = pieces[h * mp + k][...]
        _, inputs = embed_rows(id_parts[0][0:1], table[...])
        middle = inputs
        for k in range(mp):
            part = att[k * width : (k + 1) * width].astype(f32).T.astype(bf16)
            middle = middle + nn(part, out_rows(k))
        normed, inverse = layer_stats(middle)
        xhat[...] = normed
        inv[...] = inverse
        mid = normed * gain + bias
        norm_mid[...] = mid.astype(bf16)
        norm_mid_t[...] = mid.T.astype(bf16)
        total[...] = middle + down_bias

    def up_step(up, down, _):
        pre = nn(norm_mid[...], up) + vec[c, 0:1]
        value, grad = gelu_parts(pre)
        value = value.astype(bf16)
        hidden[c] = value
        slope[c] = grad
        total[...] += nn(value, down)

    chunk_step(0, up_step)

    @pl.when(step == mp - 1)
    def _():
        low = total[...].astype(bf16)
        out_low[...] = low
        block_out[...] = low
        out_low_t[...] = low.astype(f32).T.astype(bf16)
        logit[...] = jnp.zeros_like(logit)

    def pred_step(up, down, pred):
        pre = nn(out_low[...], pred) + vec[c, 1:2]
        value, grad = gelu_parts(pre)
        value = value.astype(bf16)
        p_hidden[c] = value
        p_slope[c] = grad
        logit[...] += jnp.sum(value.astype(f32) * vec[c, 2:3], axis=1, keepdims=True)

    chunk_step(1, pred_step)

    @pl.when(step == 2 * mp - 1)
    def _():
        label_rows = jnp.broadcast_to(labels[0], (128, own)).T
        label = label_rows[:, :1]
        x = logit[...] + logit_bias[...]
        fall = jnp.exp(-jnp.abs(x))
        loss = jnp.maximum(x, 0.0) + jnp.log(1.0 + fall) - label * x
        grad = jnp.where(x >= 0, 1.0, fall) / (1.0 + fall) - label
        d_scalar[0:1] = jnp.broadcast_to(jnp.sum(loss, axis=0, keepdims=True), (1, 128))
        d_scalar[1:2] = jnp.broadcast_to(jnp.sum(grad, axis=0, keepdims=True), (1, 128))
        g_logit[...] = grad.astype(bf16).astype(f32)
        total[...] = cotangent[...].astype(f32)

    def pred_back_step(up, down, pred):
        g = g_logit[...]
        g_pre = g * vec[c, 2:3] * p_slope[c]
        d_vec[place, 1:2] = jnp.sum(g_pre, axis=0, keepdims=True)
        d_vec[place, 2:3] = jnp.sum(g * p_hidden[c].astype(f32), axis=0, keepdims=True)
        g_low = g_pre.astype(bf16)
        store("pred", nn(out_low_t[...], g_low))
        total[...] += nt(g_low, pred)

    chunk_step(2, pred_back_step)

    @pl.when(step == 3 * mp - 1)
    def _():
        g_out = total[...]
        d_norm[2:3] = jnp.sum(g_out, axis=0, keepdims=True)
        grad_mid[...] = g_out
        out_low[...] = g_out.astype(bf16)
        total[...] = jnp.zeros_like(total)

    def up_back_step(up, down, _):
        g_low = out_low[...]
        store("down", tn(hidden[c], g_low))
        g_up = nt(g_low, down) * slope[c]
        d_vec[place, 0:1] = jnp.sum(g_up, axis=0, keepdims=True)
        g_up = g_up.astype(bf16)
        store("up", nn(norm_mid_t[...], g_up))
        total[...] += nt(g_up, up)

    chunk_step(3, up_back_step)

    @pl.when(step == 4 * mp - 1)
    def _():
        g_norm = total[...]
        normed = xhat[...]
        d_norm[0:1] = jnp.sum(g_norm * normed, axis=0, keepdims=True)
        d_norm[1:2] = jnp.sum(g_norm, axis=0, keepdims=True)
        g_mid = grad_mid[...] + norm_back(g_norm, normed, inv[...], gain)
        grad_mid[...] = g_mid
        g_low = g_mid.astype(bf16)
        d_att = nn(att[...], g_low)
        d_att = d_att.astype(bf16)
        out_copies = []
        for k in range(mp):
            part = d_att[k * width : (k + 1) * width]
            target = lax.rem(me - k + mp, mp)
            if dp:
                stage_out[k] = part.reshape(stage_out.shape[1:])
                rows = stage_out.shape[2]
                there = d_all.at[:, target, pl.ds(3 * stage.shape[3], rows)]
                out_copies.append(pltpu.make_async_copy(stage_out.at[k], there, sems.at[3, k]))
                out_copies[-1].start()
            else:
                d_out[target] = part
        for k in range(mp):
            part = nt(out_rows((mp - k) % mp), g_low).astype(bf16)
            for h in range(heads):
                back[h * mp + k][...] = part[h * size : (h + 1) * size]
        for copy in out_copies:
            copy.wait()
        if dp:
            for kind in kinds:
                for chunk in range(mp):
                    copy_out(kind, chunk).wait()


def rows_call(me, pieces, heads, id_parts, labels, cotangent, table, vecs, logit_bias, own_weights, weights, dp):
    mp = len(id_parts)
    size, own = pieces[0].shape
    model = table.shape[1]
    hid = own_weights[0].shape[1]
    width = heads * size

    def outer(s):
        at = jnp.where((s // mp == 0) | (s // mp == 3), lax.rem(s, mp), mp - 1)
        return jnp.maximum(at - 1, 0)

    def inner(s):
        at = jnp.where(s // mp == 0, 0, jnp.where(s // mp == 3, mp - 1, lax.rem(s, mp)))
        return jnp.maximum(at - 1, 0)

    def last(phase):
        def chunk(s, m):
            at = jnp.where(s // mp < phase, 0, jnp.where(s // mp == phase, lax.rem(s, mp), mp - 1))
            return lax.rem(m[0] - at + mp, mp)

        return lambda s, m: (chunk(s, m), 0, 0)

    outs = [jax.ShapeDtypeStruct((size, own), bf16)] * len(pieces) + [
        jax.ShapeDtypeStruct((own, model), bf16),
        jax.ShapeDtypeStruct((own, model), f32),
        jax.ShapeDtypeStruct((mp, 3, hid), f32),
        jax.ShapeDtypeStruct((3, model), f32),
        jax.ShapeDtypeStruct((2, 128), f32),
    ]
    out_specs = [full(o.shape) for o in outs]
    scratch = [
        pltpu.VMEM((mp * width, own), bf16),
        pltpu.VMEM((own, model), f32),
        pltpu.VMEM((own, 1), f32),
        pltpu.VMEM((own, model), bf16),
        pltpu.VMEM((model, own), bf16),
        pltpu.VMEM((own, model), f32),
        pltpu.VMEM((own, model), bf16),
        pltpu.VMEM((model, own), bf16),
        pltpu.VMEM((mp, own, hid), bf16),
        pltpu.VMEM((mp, own, hid), f32),
        pltpu.VMEM((mp, own, hid), bf16),
        pltpu.VMEM((mp, own, hid), f32),
        pltpu.VMEM((own, 1), f32),
        pltpu.VMEM((own, 1), f32),
        pltpu.VMEM((mp, 3, hid), f32),
    ]
    if dp:
        share, out_share = hid // dp, width // dp
        block = (dp, 1, share, model)
        weight_specs = [
            pl.BlockSpec(block, lambda s, m: (0, outer(s), 0, 0)),
            pl.BlockSpec(block, lambda s, m: (0, outer(s), 1, 0)),
            pl.BlockSpec(block, lambda s, m: (0, inner(s), 2, 0)),
            pl.BlockSpec((dp, mp - 1, out_share, model), lambda s, m: (0, 0, 3 * share // out_share, 0)),
        ]
        weights = [weights] * 4
        outs.append(jax.ShapeDtypeStruct((dp, mp, 3 * share + out_share, model), bf16))
        out_specs.append(pl.BlockSpec(memory_space=pl.ANY))
        scratch += [
            pltpu.VMEM((3, mp, dp, share, model), bf16),
            pltpu.VMEM((mp, dp, out_share, model), bf16),
            pltpu.SemaphoreType.DMA((4, mp)),
        ]
    else:
        weight_specs = [
            pl.BlockSpec((1, model, hid), lambda s, m: (outer(s), 0, 0)),
            pl.BlockSpec((1, hid, model), lambda s, m: (outer(s), 0, 0)),
            pl.BlockSpec((1, model, hid), lambda s, m: (inner(s), 0, 0)),
            full((mp - 1, width, model)),
        ]
        for phase, rows, columns in ((3, model, hid), (3, hid, model), (2, model, hid)):
            outs.append(jax.ShapeDtypeStruct((mp, rows, columns), bf16))
            out_specs.append(pl.BlockSpec((1, rows, columns), last(phase)))
        outs.append(jax.ShapeDtypeStruct((mp, width, model), bf16))
        out_specs.append(full((mp, width, model)))
    ins = [*pieces, *id_parts]
    rest = [cotangent, table, vecs, logit_bias, *own_weights]
    return pl.pallas_call(
        functools.partial(rows_kernel, mp, heads, dp),
        grid_spec=pltpu.PrefetchScalarGridSpec(
            num_scalar_prefetch=1,
            grid=(4 * mp,),
            in_specs=[full(a.shape) for a in ins]
            + [pl.BlockSpec((1, 1, own), lambda s, m: (m[0], 0, 0))]
            + [full(a.shape) for a in rest]
            + weight_specs,
            out_specs=out_specs,
            scratch_shapes=scratch,
        ),
        out_shape=outs,
        compiler_params=params(),
        cost_estimate=pl.CostEstimate(
            flops=18 * own * model * hid * mp, bytes_accessed=20 << 20, transcendentals=2 * own * hid * mp
        ),
        name="rows",
    )(me, *ins, labels, *rest, *weights)


SIDE = 64
VEC_ROWS = 24


def packed(value, model):
    side = value[:, model : model + SIDE] + value[:, model + SIDE :]
    high = side.astype(bf16)
    low = (side - high.astype(f32)).astype(bf16)
    return jnp.concatenate([value[:, :model].astype(bf16), high, low], axis=1)


def tail_kernel(mp, heads, split, me_ref, *refs):
    count = heads * mp
    pieces = refs[:count]
    own_joint, joint_rest, ids, table, vecs, grad_mid = refs[count : count + 6]
    refs = refs[count + 6 :]
    if split:
        d_norm_two, d_vec, d_scalar = refs[:3]
        d_biases = refs[3 : 3 + heads]
        grad_in, sent, kept, parts, vec_s, sums = refs[3 + heads :]
    else:
        grad_in, d_embed, d_norm, parts = refs
    me = me_ref[0]
    size = pieces[0].shape[0] // 3
    width = heads * size
    for h in range(heads):
        for k in range(mp):
            for kind in range(3):
                row = (k * 3 + kind) * width + h * size
                parts[row : row + size] = pieces[h * mp + k][kind * size : (kind + 1) * size]
    g_norm = tn(parts[: 3 * width], own_joint[...])
    for k in range(1, mp):
        part = parts[k * 3 * width : (k + 1) * 3 * width]
        g_norm = g_norm + tn(part, joint_rest[:, k - 1].reshape(3 * width, -1))
    one_hot_t, inputs = embed_rows(ids[0:1], table[...])
    normed, inverse = layer_stats(inputs)
    d_gain = jnp.sum(g_norm * normed, axis=0, keepdims=True)
    d_bias = jnp.sum(g_norm, axis=0, keepdims=True)
    g_in = grad_mid[...] + norm_back(g_norm, normed, inverse, vecs[0:1])
    first = g_in.astype(bf16)
    grad_in[...] = first
    rest = g_in - first.astype(f32)
    second = rest.astype(bf16)
    third = (rest - second.astype(f32)).astype(bf16)
    hot = one_hot_t.astype(bf16)
    embed = nn(hot, first) + nn(hot, second) + nn(hot, third)
    if not split:
        d_embed[...] = embed
        d_norm[0:1] = d_gain
        d_norm[1:2] = d_bias
        return
    model = grad_mid.shape[1]
    vec_s[...] = jnp.zeros_like(vec_s)
    vec_s[0:1] = d_gain
    vec_s[1:2] = d_bias
    vec_s[2:5] = d_norm_two[...]
    for z in range(mp):
        vec_s[5 + 3 * z : 8 + 3 * z] = d_vec[z]
    sums[:, :model] = embed
    sums[:, model:] = jnp.zeros((sums.shape[0], 2 * SIDE), f32)
    for g in range(model // SIDE):
        sums[g * VEC_ROWS : (g + 1) * VEC_ROWS, model : model + SIDE] = vec_s[
            :, g * SIDE : (g + 1) * SIDE
        ]
    start = VEC_ROWS * (model // SIDE)
    for z in range(mp):
        for h in range(heads):
            row = start + 8 * z + 2 * h
            for kind in range(2):
                values = d_biases[h][0:1, kind * size : (kind + 1) * size]
                sums[row + kind : row + kind + 1, model : model + SIDE] = jnp.where(me == z, values, 0.0)
    row = start + 8 * mp
    sums[row : row + 2, model : model + SIDE] = d_scalar[:, :SIDE]
    half = kept.shape[0]
    core = lax.rem(me_ref[1], 2)
    kept[...] = sums[pl.ds(pl.multiple_of(core * half, half), half)]
    sent[...] = packed(sums[pl.ds(pl.multiple_of((1 - core) * half, half), half)], model)


def tail_call(me, pieces, heads, own_joint, joint_rest, ids, table, vecs, grad_mid, smalls):
    mp = len(pieces) // heads
    own, model = grad_mid.shape
    vocab = table.shape[0]
    wide = model + 2 * SIDE
    outs = [jax.ShapeDtypeStruct((own, model), bf16)]
    scratch = [pltpu.VMEM((mp * own_joint.shape[0], own), bf16)]
    if smalls:
        outs += [
            jax.ShapeDtypeStruct((vocab // 2, wide), bf16),
            jax.ShapeDtypeStruct((vocab // 2, wide), f32),
        ]
        scratch += [pltpu.VMEM((VEC_ROWS, model), f32), pltpu.VMEM((vocab, wide), f32)]
    else:
        outs += [jax.ShapeDtypeStruct(table.shape, f32), jax.ShapeDtypeStruct((2, model), f32)]
    ins = [*pieces, own_joint, joint_rest, ids, table, vecs, grad_mid, *smalls]
    return grid_call(
        functools.partial(tail_kernel, mp, heads, bool(smalls)), "tail", me, ins, outs, scratch
    )


def grid_call(kernel, name, me, ins, outs, scratch=()):
    return pl.pallas_call(
        kernel,
        grid_spec=pltpu.PrefetchScalarGridSpec(
            num_scalar_prefetch=1,
            grid=(1,),
            in_specs=[full(a.shape) for a in ins],
            out_specs=[full(o.shape) for o in outs],
            scratch_shapes=list(scratch),
        ),
        out_shape=outs,
        compiler_params=params(),
        cost_estimate=pl.CostEstimate(
            flops=1 << 28,
            bytes_accessed=sum(math.prod(a.shape) * a.dtype.itemsize for a in [*ins, *outs]),
            transcendentals=0,
        ),
        name=name,
    )(me, *ins)


def whole_call(kernel, name, me, ins, outs, scratch=()):
    vmem = pl.BlockSpec(memory_space=pltpu.VMEM)
    return pl.pallas_call(
        kernel,
        in_specs=[pl.BlockSpec(memory_space=pltpu.SMEM)] + [vmem] * len(ins),
        out_specs=[vmem] * len(outs),
        out_shape=outs,
        scratch_shapes=list(scratch),
        compiler_params=pltpu.CompilerParams(vmem_limit_bytes=SMALL_VMEM_BYTES),
        cost_estimate=pl.CostEstimate(
            flops=1 << 20,
            bytes_accessed=sum(math.prod(a.shape) * a.dtype.itemsize for a in [*ins, *outs]),
            transcendentals=0,
        ),
        name=name,
    )(me, *ins)


def shift_pairs(count, k):
    return [(s, (s + k) % count) for s in range(count)]


def exchange(parts, axis, count):
    return [parts[0]] + [
        lax.ppermute(parts[k], axis, shift_pairs(count, k)) for k in range(1, count)
    ]


def swap(value, dp, bits):
    return lax.ppermute(value, "dp", [(s, s ^ bits) for s in range(dp)])


def plane_of(me_ref):
    return me_ref[1] // 2


def halves_kernel(planes, model, me_ref, kept, got, own_out, *sends):
    rows = own_out.shape[0]
    mine = plane_of(me_ref)
    for k in range(planes):
        place = pl.ds(pl.multiple_of(jnp.bitwise_xor(mine, k) * rows, rows), rows)
        value = kept[place].astype(f32) + got[place].astype(f32)
        if k == 0:
            own_out[...] = value
        elif model:
            sends[k - 1][...] = packed(value, model)
        else:
            sends[k - 1][...] = value.astype(bf16)


def halves_call(me, kept, got, planes, model):
    rows, wide = kept.shape[0] // planes, kept.shape[1]
    outs = [jax.ShapeDtypeStruct((rows, wide), f32)]
    outs += [jax.ShapeDtypeStruct((rows, wide), bf16)] * (planes - 1)
    return whole_call(
        functools.partial(halves_kernel, planes, model), "add_halves", me, [kept, got], outs
    )


def plane_kernel(model, me_ref, own, *refs):
    value = own[...]
    for ref in refs[:-1]:
        value = value + ref[...].astype(f32)
    refs[-1][...] = packed(value, model)


def line_kernel(mp, model, me_ref, *refs):
    parts, out, held = refs[:mp], refs[mp], refs[mp + 1]
    me = me_ref[0]
    for k in range(mp):
        held[lax.rem(me - k + mp, mp)] = parts[k][...]
    value = held[0].astype(f32)
    for z in range(1, mp):
        value = value + held[z].astype(f32)
    out[...] = packed(value, model)


def join_kernel(planes, me_ref, *refs):
    parts, out = refs[:planes], refs[planes]
    rows = parts[0].shape[0]
    mine = plane_of(me_ref)
    for k in range(planes):
        place = pl.ds(pl.multiple_of(jnp.bitwise_xor(mine, k) * rows, rows), rows)
        out[place] = parts[k][...]


def small_kernel(mp, heads, size, scale, me_ref, mine, other, *refs):
    d_embed, gain1, bias1, gain2, bias2, down, up_b, pred_b, logit_w, cb, pb, loss, logit_b, held, vec_s = refs
    half = mine.shape[0]
    core = lax.rem(me_ref[1], 2)
    held[pl.ds(pl.multiple_of(core * half, half), half)] = mine[...].astype(f32)
    held[pl.ds(pl.multiple_of((1 - core) * half, half), half)] = other[...].astype(f32)
    model = d_embed.shape[1]
    d_embed[...] = held[:, :model]
    side = held[:, model : model + SIDE] + held[:, model + SIDE :]
    for g in range(model // SIDE):
        vec_s[:, g * SIDE : (g + 1) * SIDE] = side[g * VEC_ROWS : (g + 1) * VEC_ROWS]
    for place, ref in enumerate((gain1, bias1, gain2, bias2, down)):
        ref[...] = vec_s[place : place + 1]
    me = me_ref[0]
    start = VEC_ROWS * (model // SIDE)
    for place, ref in enumerate((up_b, pred_b, logit_w)):
        value = vec_s[5 + place : 6 + place]
        for z in range(1, mp):
            value = jnp.where(me == z, vec_s[5 + 3 * z + place : 6 + 3 * z + place], value)
        ref[...] = value
    for h in range(heads):
        for kind, ref in enumerate((cb, pb)):
            row = start + 2 * h + kind
            value = side[row : row + 1]
            for z in range(1, mp):
                value = jnp.where(me == z, side[row + 8 * z : row + 8 * z + 1], value)
            ref[h : h + 1] = value[:, :size]
    row = start + 8 * mp
    loss[...] = side[row : row + 1, :1] * scale
    logit_b[...] = side[row + 1 : row + 2, :1]


def sum_small(me, sent, kept, dp, mp, model):
    planes = dp // 2
    got = swap(sent, dp, 1)
    own, *sends = halves_call(me, kept, got, planes, model)
    got = [swap(sends[k - 1], dp, 2 * k) for k in range(1, planes)]
    piece = jax.ShapeDtypeStruct(own.shape, bf16)
    (part,) = whole_call(functools.partial(plane_kernel, model), "add_plane", me, [own, *got], [piece])
    got = exchange([part] * mp, "mp", mp)
    (part,) = whole_call(
        functools.partial(line_kernel, mp, model),
        "add_line",
        me,
        got,
        [piece],
        [pltpu.VMEM((mp, *own.shape), bf16)],
    )
    got = [part] + [swap(part, dp, 2 * k) for k in range(1, planes)]
    return got


def spread_small(me, got, dp, mp, heads, size):
    planes = dp // 2
    rows, wide = got[0].shape
    model = wide - 2 * SIDE
    half = jax.ShapeDtypeStruct((planes * rows, wide), bf16)
    (mine,) = whole_call(functools.partial(join_kernel, planes), "join", me, got, [half])
    other = swap(mine, dp, 1)
    vocab = 2 * planes * rows
    row = jax.ShapeDtypeStruct((1, model), f32)
    one = jax.ShapeDtypeStruct((1, 1), f32)
    by_head = jax.ShapeDtypeStruct((heads, size), f32)
    outs = [jax.ShapeDtypeStruct((vocab, model), f32)] + [row] * 8 + [by_head] * 2 + [one] * 2
    return whole_call(
        functools.partial(small_kernel, mp, heads, size, 1.0 / (LEN * dp)),
        "small_sums",
        me,
        [mine, other],
        outs,
        [pltpu.VMEM((vocab, wide), f32), pltpu.VMEM((VEC_ROWS, model), f32)],
    )


def heads_kernel(heads, pieces, me_ref, *refs):
    joints, poses = refs[:heads], refs[heads : 2 * heads]
    kept, sent, joint, pos = refs[2 * heads :]
    size = joints[0].shape[0] // 3
    width = heads * size
    for h in range(heads):
        for kind in range(3):
            row = kind * width + h * size
            joint[row : row + size] = joints[h][kind * size : (kind + 1) * size]
    value = poses[0][...]
    lane = lax.broadcasted_iota(jnp.int32, value.shape, 1)
    for h in range(1, heads):
        value = jnp.where(lane >= h * size, poses[h][...], value)
    pos[...] = value.astype(bf16)
    groups = joint.shape[1] // width
    j_rows = joint.shape[0] // pieces
    p_rows = pos.shape[0] // pieces // groups
    rows = j_rows + p_rows
    core = lax.rem(me_ref[1], 2)
    for piece in range(pieces):
        block = [joint[piece * j_rows : (piece + 1) * j_rows]]
        start = piece * p_rows * groups
        spread = [pos[start + g * p_rows : start + (g + 1) * p_rows] for g in range(groups)]
        block.append(jnp.concatenate(spread, axis=1))
        at = (piece % (pieces // 2)) * rows

        @pl.when(core == piece // (pieces // 2))
        def _(at=at, block=block):
            kept[at : at + j_rows] = block[0]
            kept[at + j_rows : at + rows] = block[1]

        @pl.when(core != piece // (pieces // 2))
        def _(at=at, block=block):
            sent[at : at + j_rows] = block[0]
            sent[at + j_rows : at + rows] = block[1]


def lines_kernel(mp, me_ref, *refs):
    count = len(refs) - mp
    (part,), outs = refs[:count], refs[count:]
    me = me_ref[0]
    for k in range(mp):
        outs[k][...] = part[lax.rem(me + k, mp)]


def merge_kernel(mp, me_ref, *refs):
    lines, own, planes, out = refs[:mp], refs[mp], refs[mp + 1 : -1], refs[-1]
    value = lines[0][...].astype(f32)
    for k in range(1, mp):
        value = value + lines[k][...].astype(f32)
    rows = value.shape[0]
    out[:rows] = value.astype(bf16)
    value = own[...]
    for ref in planes:
        value = value + ref[...].astype(f32)
    out[rows:] = value.astype(bf16)


def spread_kernel(order, dp, me_ref, *refs):
    parts = refs[:dp]
    up, down, pred, out, query, key, value, pos, joint = refs[dp:]
    mine = me_ref[1]
    planes = dp // 2
    groups = joint.shape[1] // pos.shape[1]
    for bits, part in zip(order, parts):
        source = jnp.bitwise_xor(mine, bits)
        row = 0
        for ref in (up, down, pred, out):
            rows = ref.shape[0] // dp
            ref[pl.ds(pl.multiple_of(source * rows, rows), rows)] = part[row : row + rows].astype(f32)
            row += rows
        piece = lax.rem(source, 2) * planes + source // 2
        rows = joint.shape[0] // dp
        joint[pl.ds(pl.multiple_of(piece * rows, rows), rows)] = part[row : row + rows].astype(f32)
        row += rows
        rows = pos.shape[0] // dp // groups
        width = pos.shape[1]
        for g in range(groups):
            place = pl.multiple_of((piece * groups + g) * rows, rows)
            pos[pl.ds(place, rows)] = part[row : row + rows, g * width : (g + 1) * width].astype(f32)
    width = pos.shape[1]
    for kind, ref in enumerate((query, key, value)):
        ref[...] = joint[kind * width : (kind + 1) * width].T


def sum_weights(me, grads, first, after, joints, poses, dp, mp):
    planes = dp // 2
    model = joints[0].shape[1]
    width = poses[0].shape[1]
    summed = lax.psum_scatter(grads, "dp", scatter_dimension=0, tiled=True)
    summed, *_ = lax.optimization_barrier((summed.reshape(mp, -1, model), *first))
    piece_rows = summed.shape[1]
    piece = jax.ShapeDtypeStruct((piece_rows, model), bf16)
    line = whole_call(functools.partial(lines_kernel, mp), "cut_lines", me, [summed], [piece] * mp)
    line = exchange(line, "mp", mp)
    half_rows = (3 * width + model * width // model) // 2
    half = jax.ShapeDtypeStruct((half_rows, model), bf16)
    kept, sent = grid_call(
        functools.partial(heads_kernel, len(joints), dp),
        "cut_heads",
        me,
        [*joints, *poses],
        [half, half],
        [pltpu.VMEM((3 * width, model), bf16), pltpu.VMEM((model, width), bf16)],
    )
    got = swap(sent, dp, 1)
    own, *sends = halves_call(me, kept, got, planes, 0)
    got = [swap(sends[k - 1], dp, 2 * k) for k in range(1, planes)]
    *line, _ = lax.optimization_barrier((*line, after))
    (part,) = whole_call(
        functools.partial(merge_kernel, mp),
        "merge",
        me,
        [*line, own, *got],
        [jax.ShapeDtypeStruct((piece_rows + own.shape[0], model), bf16)],
    )
    order, parts = [], []
    for k in range(planes):
        there = swap(part, dp, 2 * k) if k else part
        order += [2 * k, 2 * k + 1]
        parts += [there, swap(there, dp, 1)]
    square = jax.ShapeDtypeStruct((model, model), f32)
    thin = jax.ShapeDtypeStruct((model, width), f32)
    outs = [square] * 3 + [jax.ShapeDtypeStruct((width, model), f32)] + [thin] * 4
    return whole_call(
        functools.partial(spread_kernel, order, dp),
        "spread",
        me,
        parts,
        outs,
        [pltpu.VMEM((3 * width, model), f32)],
    )


def per_device(
    byte_ids,
    embed_table,
    boundary_labels,
    out_cotangent,
    norm_one_gain,
    norm_one_bias,
    w_query,
    w_key,
    w_value,
    w_position,
    content_bias,
    position_bias,
    w_out,
    norm_two_gain,
    norm_two_bias,
    w_up,
    up_bias,
    w_down,
    down_bias,
    w_pred,
    pred_bias,
    w_logit,
    logit_bias,
):
    dp, mp = lax.axis_size("dp"), lax.axis_size("mp")
    me_dp, me_mp = lax.axis_index("dp"), lax.axis_index("mp")
    own = byte_ids.shape[0]
    assert boundary_labels.shape[0] == LEN and own * mp == LEN and w_up.shape[1] == own
    model = embed_table.shape[1]
    vocab = embed_table.shape[0]
    heads, size = content_bias.shape
    width = heads * size
    hid = w_up.shape[1]
    scale = 1.0 / math.sqrt(size)
    planned = (
        hid == model
        and size == SIDE
        and dp & (dp - 1) == 0
        and width % (16 * dp) == 0
        and vocab % (16 * dp) == 0
        and VEC_ROWS * (model // SIDE) + 8 * mp + 2 <= vocab
        and 5 + 3 * mp <= VEC_ROWS
        and 2 * heads <= 8
    )
    me = jnp.stack([me_mp, me_dp]).astype(jnp.int32)
    own_weights = (w_up, w_down, w_pred, w_out)
    shorts = [byte_ids, up_bias, pred_bias, w_logit, norm_one_gain, norm_one_bias, norm_two_gain, norm_two_bias]
    shorts += [down_bias, content_bias, position_bias, logit_bias, boundary_labels]
    shorts += [w_query, w_key, w_value, w_position]
    prepared = prep_call(me, shorts, own_weights, mp, dp if planned else 0)
    head_rows, vecs, biases, labels, logit_row, w_joint, w_pos_t, joint_t = prepared[:8]

    id_parts = exchange([head_rows] * mp, "mp", mp)

    if planned:
        *id_parts, shares = lax.optimization_barrier((*id_parts, prepared[8]))
        shares = exchange([shares] * mp, "mp", mp)[1:]
    else:
        weights = [jnp.stack(exchange([w] * mp, "mp", mp)[1:]) for w in own_weights]
        joint_rest = jnp.stack(exchange([joint_t] * mp, "mp", mp)[1:])[None]

    sin_np, cos_np = feature_tables(model)
    feature = np.concatenate([cos_np, sin_np], axis=1).astype(jnp.bfloat16)
    tables = (
        jnp.asarray(feature),
        jnp.asarray(np.ascontiguousarray(feature.T)),
        jnp.asarray(sin_np),
        jnp.asarray(cos_np),
    )
    tables_t = (
        jnp.asarray(np.ascontiguousarray(sin_np.T)),
        jnp.asarray(np.ascontiguousarray(cos_np.T)),
    )

    norm_all, qcat, kcat, kcat_t, v, v_t, shift = pre_call(
        me,
        id_parts,
        embed_table,
        vecs,
        w_joint,
        w_position,
        biases,
        tables,
        heads,
        scale,
    )
    if planned:
        qcat, *shares = lax.optimization_barrier((qcat, *shares))
        shares = jnp.stack(shares)
        cut = shares.shape[1] - 3 * width // dp
        weights = lax.all_gather(shares[:, :cut], "dp", axis=0, tiled=False)
    saved, sent = [], []
    for h in range(heads):
        if h:
            qcat, _ = lax.optimization_barrier((qcat, inv))
        expon, full_t, inv, *parts = fwd_call(me, h, qcat, kcat, v_t, mp, own, size)
        saved.append((expon, full_t, inv))
        sent += exchange(parts, "mp", mp)

    if planned:
        *sent, joint_rest = lax.optimization_barrier((*sent, shares[:, cut:]))
        joint_rest = lax.all_gather(joint_rest, "dp", axis=0, tiled=False)
    result = rows_call(
        me,
        sent,
        heads,
        id_parts,
        labels,
        out_cotangent,
        embed_table,
        vecs,
        logit_row,
        own_weights,
        weights,
        dp if planned else 0,
    )
    back = result[: heads * mp]
    block_out, grad_mid, d_vec, d_norm_two, d_scalar, *d_weights = result[heads * mp :]

    if planned:
        d_weights[0], joint_rest = lax.optimization_barrier((d_weights[0], joint_rest))
    arrived, d_joint, d_pos, d_bias = [], [], [], []
    for h in range(heads):
        pieces = exchange(back[h * mp : (h + 1) * mp], "mp", mp)
        if h:
            qcat, _ = lax.optimization_barrier((qcat, parts[0]))
        parts = bwd_call(
            me,
            h,
            heads,
            pieces,
            *saved[h],
            qcat,
            kcat_t,
            v,
            shift,
            w_pos_t,
            tables_t,
            norm_all,
            scale,
        )
        arrived += exchange(parts[:mp], "mp", mp)
        d_joint.append(parts[mp])
        d_pos.append(parts[mp + 1])
        d_bias.append(parts[mp + 2])
    smalls = [d_norm_two, d_vec, d_scalar, *d_bias] if planned else []
    arrived = list(lax.optimization_barrier(tuple(arrived)))
    grad_input, *rest = tail_call(
        me, arrived, heads, joint_t, joint_rest, head_rows, embed_table, vecs, grad_mid, smalls
    )

    if planned:
        small = sum_small(me, *rest, dp, mp, model)
        up, down, pred, out, query, key, value, pos = sum_weights(
            me, d_weights[0], rest, small[0], d_joint, d_pos, dp, mp
        )
        (embed, gain1, bias1, gain2, bias2, down_b, up_b, pred_b, logit_w, cb, pb, loss, logit_b) = spread_small(
            me, small, dp, mp, heads, size
        )
    else:
        d_embed, d_norm_one = rest

        def shard_sum(value):
            summed = lax.psum(value, ("dp", "mp"))
            return lax.dynamic_index_in_dim(summed, me_mp, 0, keepdims=False).astype(f32)

        up, down, pred, out = [shard_sum(g) for g in d_weights]
        up_b, pred_b, logit_w = shard_sum(d_vec)
        joint = lax.psum(jnp.stack(d_joint), "dp").astype(f32)
        joint = joint.reshape(heads, 3, size, model).transpose(1, 3, 0, 2).reshape(3, model, width)
        query, key, value = joint
        pos = jnp.concatenate(
            [d_pos[h][:, h * size : (h + 1) * size] for h in range(heads)], axis=1
        )
        pos = lax.psum(pos.astype(bf16), "dp").astype(f32)
        biases = lax.psum(jnp.stack([d[0] for d in d_bias]), "dp")
        cb, pb = biases[:, :size], biases[:, size:]
        embed, norm_one, norm_two, scalars = lax.psum(
            (d_embed, d_norm_one, d_norm_two, d_scalar), ("dp", "mp")
        )
        gain1, bias1 = norm_one
        gain2, bias2, down_b = norm_two
        loss = scalars[0, :1] / (LEN * dp)
        logit_b = scalars[1, :1]
    flat = lambda v: v.reshape(-1)
    return (
        block_out,
        flat(loss),
        grad_input,
        embed,
        flat(gain1),
        flat(bias1),
        query,
        key,
        value,
        pos,
        cb,
        pb,
        out,
        flat(gain2),
        flat(bias2),
        up,
        flat(up_b),
        down,
        flat(down_b),
        pred,
        flat(pred_b),
        flat(logit_w),
        flat(logit_b),
    )


def solution(mesh):
    by_rows = P(("dp", "mp"), None)
    columns = P(None, "mp")
    shard = P("mp", None)
    placed = (
        P(("dp", "mp")),
        P(),
        P("dp"),
        by_rows,
        P(),
        P(),
        columns,
        columns,
        columns,
        columns,
        shard,
        shard,
        shard,
        P(),
        P(),
        columns,
        P("mp"),
        shard,
        P(),
        columns,
        P("mp"),
        P("mp"),
        P(),
    )
    results = (
        by_rows,
        P(),
        by_rows,
        P(),
        P(),
        P(),
        columns,
        columns,
        columns,
        columns,
        shard,
        shard,
        shard,
        P(),
        P(),
        columns,
        P("mp"),
        shard,
        P(),
        columns,
        P("mp"),
        P("mp"),
        P(),
    )
    return jax.shard_map(
        per_device, mesh=mesh, in_specs=placed, out_specs=results, check_vma=False
    )
```

```python
import functools
import math

import jax
import jax.numpy as jnp
import numpy as np
from jax import lax
from jax.experimental import pallas as pl
from jax.experimental.pallas import tpu as pltpu
from jax.sharding import PartitionSpec as P

LEN = 2048
BLOCK = 256
CHUNK = 512
VMEM_BYTES = 56 * 1024 * 1024
SMALL_VMEM_BYTES = 20 * 1024 * 1024

bf16 = jnp.bfloat16
f32 = jnp.float32
norm_eps = 1e-05
density_scale = 1.0 / math.sqrt(2.0 * math.pi)
log2_e = math.log2(math.e)


def nn(first, second):
    return jnp.dot(first, second, preferred_element_type=f32)


def nt(first, second):
    return lax.dot_general(
        first, second, (((1,), (1,)), ((), ())), preferred_element_type=f32
    )


def tn(first, second):
    return lax.dot_general(
        first, second, (((0,), (0,)), ((), ())), preferred_element_type=f32
    )


def layer_stats(values):
    centered = values - jnp.mean(values, axis=-1, keepdims=True)
    inverse = lax.rsqrt(jnp.mean(centered * centered, axis=-1, keepdims=True) + norm_eps)
    return centered * inverse, inverse


def norm_back(grad_normed, normed, inverse, gain_row):
    scaled = grad_normed * gain_row
    first_mean = jnp.mean(scaled, axis=-1, keepdims=True)
    second_mean = jnp.mean(scaled * normed, axis=-1, keepdims=True)
    return inverse * (scaled - first_mean - normed * second_mean)


def gelu_parts(values):
    size = jnp.abs(values)
    density = jnp.exp2(values * values * (-0.5 * log2_e) + math.log2(density_scale))
    below = 1.0 + (0.3275911 / math.sqrt(2.0)) * size
    t = pl.reciprocal(below, approx=True)
    t = t * (2.0 - below * t)
    fold = 0.5 / density_scale
    poly = (1.061405429 * fold) * t - 1.453152027 * fold
    poly = poly * t + 1.421413741 * fold
    poly = poly * t - 0.284496736 * fold
    poly = poly * t + 0.254829592 * fold
    tail = poly * t * density
    phi = jnp.where(values >= 0, 1.0 - tail, tail)
    return jnp.maximum(values, 0.0) - size * tail, phi + values * density


def feature_tables(model_width):
    half = model_width // 2
    frequency = np.exp(
        np.arange(half, dtype=np.float64) * (-2.0 * math.log(10000.0) / model_width)
    )
    angles = np.arange(LEN, dtype=np.float64)[:, None] * frequency[None, :]
    sin, cos = np.sin(angles), np.cos(angles)
    feature = np.concatenate([cos, sin], axis=1).astype(jnp.bfloat16)
    turn = np.concatenate([sin[:BLOCK], cos[:BLOCK]], axis=1).astype(np.float32)
    turn_block = np.concatenate([sin[::BLOCK], cos[::BLOCK]], axis=0).astype(np.float32)
    return feature, turn, turn_block


def embed_rows(ids_row, table):
    vocab = table.shape[0]
    places = lax.broadcasted_iota(jnp.int32, (vocab, ids_row.shape[1]), 0)
    one_hot_t = (places == ids_row.astype(jnp.int32)).astype(f32)
    rows = nn(one_hot_t.T.astype(bf16), table)
    return one_hot_t, rows


def full(shape):
    return pl.BlockSpec(shape, lambda *_: (0,) * len(shape))


def params():
    return pltpu.CompilerParams(vmem_limit_bytes=VMEM_BYTES)


def prep_kernel(dp, me_ref, *refs):
    (ids, up_bias, pred_bias, w_logit, gain1, bias1, gain2, bias2, down_bias, cb, pb, logit_bias, labels) = refs[:13]
    w_query, w_key, w_value, w_pos = refs[13:17]
    weights = refs[17:21] if dp else ()
    out = refs[17 + len(weights) :]
    head_rows, vecs, biases, label_rows, logit_b, w_joint, w_pos_t, joint_t = out[:8]
    copies = []
    width = w_query.shape[1]
    for place, ref in enumerate((w_query, w_key, w_value)):
        w_joint[:, place * width : (place + 1) * width] = ref[...]
        joint_t[place * width : (place + 1) * width] = ref[...].astype(f32).T.astype(bf16)
    if dp:
        shares, sems = out[8:]
        row = 0
        for place, ref in enumerate(weights):
            rows = ref.shape[0] // dp
            start = pl.multiple_of(me_ref[1] * rows, rows)
            copy = pltpu.make_async_copy(
                ref.at[pl.ds(start, rows)], shares.at[pl.ds(row, rows)], sems.at[place]
            )
            copy.start()
            copies.append(copy)
            row += rows
        rows = joint_t.shape[0] // dp
        start = pl.multiple_of(me_ref[1] * rows, rows)
        shares[row : row + rows] = joint_t[pl.ds(start, rows)]
    own = ids.shape[0]
    row_of = lambda ref: ref[...].astype(f32).reshape(1, -1)
    head_rows[...] = jnp.zeros_like(head_rows)
    for place, ref in enumerate((ids, up_bias, pred_bias, w_logit)):
        head_rows[place : place + 1] = row_of(ref).astype(bf16)
    vecs[...] = jnp.zeros_like(vecs)
    for place, ref in enumerate((gain1, bias1, gain2, bias2, down_bias)):
        vecs[place : place + 1] = row_of(ref)
    heads = cb.shape[0]
    for place, ref in enumerate((cb, pb)):
        rows = [ref[h : h + 1].astype(f32) for h in range(heads)]
        biases[place : place + 1] = jnp.concatenate(rows, axis=1) if heads > 1 else rows[0]
    for z in range(label_rows.shape[0]):
        label_rows[z] = labels[z * own : (z + 1) * own].astype(f32).reshape(1, own)
    logit_b[...] = logit_bias[...].astype(f32).reshape(1, 1)
    w_pos_t[...] = w_pos[...].astype(f32).T.astype(bf16)
    for copy in copies:
        copy.wait()


def prep_call(me, ins, weights, mp, dp):
    own, vec = ins[0].shape[0], ins[4].shape[0]
    width = ins[13].shape[1]
    outs = [
        jax.ShapeDtypeStruct((16, own), bf16),
        jax.ShapeDtypeStruct((8, vec), f32),
        jax.ShapeDtypeStruct((2, width), f32),
        jax.ShapeDtypeStruct((mp, 1, own), f32),
        jax.ShapeDtypeStruct((1, 1), f32),
        jax.ShapeDtypeStruct((vec, 3 * width), bf16),
        jax.ShapeDtypeStruct((width, vec), bf16),
        jax.ShapeDtypeStruct((3 * width, vec), bf16),
    ]
    scratch = []
    if dp:
        rows = (sum(w.shape[0] for w in weights) + 3 * width) // dp
        outs.append(jax.ShapeDtypeStruct((rows, vec), bf16))
        scratch = [pltpu.SemaphoreType.DMA((len(weights),))]
        ins = [*ins, *weights]
    return pl.pallas_call(
        functools.partial(prep_kernel, dp),
        grid_spec=pltpu.PrefetchScalarGridSpec(
            num_scalar_prefetch=1,
            grid=(1,),
            in_specs=[full(a.shape) for a in ins[:17]]
            + [pl.BlockSpec(memory_space=pl.ANY)] * (len(ins) - 17),
            out_specs=[full(o.shape) for o in outs],
            scratch_shapes=scratch,
        ),
        out_shape=outs,
        compiler_params=params(),
        name="prepare",
    )(me, *ins)


def pre_kernel(mp, heads, score_scale, me_ref, *refs):
    id_refs = refs[:mp]
    (table, vecs, w_joint, w_pos, biases, turn, turn_block) = refs[mp : mp + 7]
    norm_out, posq, slot, k_out, k_t, v_out, v_t, shift_out, ids_s = refs[mp + 7 :]
    step = pl.program_id(0)
    me = me_ref[0]
    own = id_refs[0].shape[1]

    @pl.when(step == 0)
    def _():
        for k in range(mp):
            source = lax.rem(me - k + mp, mp)
            ids_s[:, pl.ds(pl.multiple_of(source * own, own), own)] = id_refs[k][0:1].astype(f32)

    rows = norm_out.shape[0]
    ids = ids_s[:, pl.ds(pl.multiple_of(step * rows, rows), rows)]
    _, inputs = embed_rows(ids, table[...])
    normed, _ = layer_stats(inputs)
    norm_in = (normed * vecs[0:1] + vecs[1:2]).astype(bf16)
    norm_out[...] = norm_in
    joint = nn(norm_in, w_joint[...])
    width = v_out.shape[1]
    head_size = width // heads
    raw = joint[:, :width]
    keys = joint[:, width : 2 * width].astype(bf16)
    values = joint[:, 2 * width :].astype(bf16)
    v_out[...] = values
    v_t[...] = values.astype(f32).T.astype(bf16)
    half = norm_in.shape[1] // 2
    k_out[...] = keys
    k_t[...] = keys.astype(f32).T.astype(bf16)
    shift = (raw + biases[1:2]).astype(bf16)
    shift_out[...] = shift
    fold = score_scale * log2_e
    content = (raw + biases[0:1]) * fold
    lane = lax.broadcasted_iota(jnp.int32, content.shape, 1)
    blocks = turn_block.shape[0] // 2
    sin_a, cos_a = turn_block[pl.ds(step, 1)], turn_block[pl.ds(blocks + step, 1)]
    sin_r, cos_r = turn[:, :half], turn[:, half:]
    sin = sin_a * cos_r + cos_a * sin_r
    cos = cos_a * cos_r - sin_a * sin_r
    for h in range(heads):
        low, high = h * head_size, (h + 1) * head_size
        coeffs = nt(shift[:, low:high], w_pos[:, low:high])
        c_sin, c_cos = coeffs[:, :half] * fold, coeffs[:, half:] * fold
        posq[h, :, :half] = (c_sin * sin + c_cos * cos).astype(bf16)
        posq[h, :, half:] = (c_cos * sin - c_sin * cos).astype(bf16)
        mine = (lane >= low) & (lane < high)
        slot[h] = jnp.where(mine, content, 0.0).astype(bf16)


def pre_call(me, id_parts, table, vecs, w_joint, w_pos, biases, turns, heads, scale):
    mp = len(id_parts)
    own = id_parts[0].shape[1]
    model = table.shape[1]
    width = w_pos.shape[1]
    rows = BLOCK
    row_block = lambda n: pl.BlockSpec((rows, n), lambda i, m: (i, 0))
    col_block = lambda n: pl.BlockSpec((n, rows), lambda i, m: (0, i))
    ins = [*id_parts, table, vecs, w_joint, w_pos, biases, *turns]
    return pl.pallas_call(
        functools.partial(pre_kernel, mp, heads, scale),
        grid_spec=pltpu.PrefetchScalarGridSpec(
            num_scalar_prefetch=1,
            grid=(LEN // rows,),
            in_specs=[full(a.shape) for a in ins],
            out_specs=[
                row_block(model),
                pl.BlockSpec((heads, rows, model), lambda i, m: (0, i, 0)),
                pl.BlockSpec((heads, rows, width), lambda i, m: (0, i, 0)),
                row_block(width),
                col_block(width),
                row_block(width),
                col_block(width),
                row_block(width),
            ],
            scratch_shapes=[pltpu.VMEM((1, mp * own), f32)],
        ),
        out_shape=[
            jax.ShapeDtypeStruct((LEN, model), bf16),
            jax.ShapeDtypeStruct((heads, LEN, model), bf16),
            jax.ShapeDtypeStruct((heads, LEN, width), bf16),
            jax.ShapeDtypeStruct((LEN, width), bf16),
            jax.ShapeDtypeStruct((width, LEN), bf16),
            jax.ShapeDtypeStruct((LEN, width), bf16),
            jax.ShapeDtypeStruct((width, LEN), bf16),
            jax.ShapeDtypeStruct((LEN, width), bf16),
        ],
        compiler_params=params(),
        cost_estimate=pl.CostEstimate(
            flops=2 * LEN * model * (table.shape[0] + 4 * width), bytes_accessed=24 << 20, transcendentals=0
        ),
        name="project",
    )(me, *ins)


def chunk_list(extent, step=CHUNK):
    return [(low, min(low + step, extent)) for low in range(0, extent, step)]


def fwd_kernel(mp, own, me_ref, posq, slot, feature, k, v_t, expon, full_t, inv_out, *refs):
    piece_refs = refs[:mp]
    key_s, query_s, exp_s, score_s, mixed_s, in_sem, out_sem = refs[mp:]
    me = me_ref[0]
    heads, blocks, _, rows = expon.shape
    model = feature.shape[1]
    width = k.shape[1]
    size = width // heads
    slots = exp_s.shape[0]

    def load(block):
        part = pl.ds(block * rows, rows)
        wide, narrow = pl.ds(0, model), pl.ds(model, width)
        pairs = [(feature.at[part], key_s.at[part, wide]), (k.at[part], key_s.at[part, narrow])]
        for h in range(heads):
            pairs.append((posq.at[h, part], query_s.at[h, part, wide]))
            pairs.append((slot.at[h, part], query_s.at[h, part, narrow]))
        return [
            pltpu.make_async_copy(source, target, in_sem.at[block, place])
            for place, (source, target) in enumerate(pairs)
        ]

    items = [(block, h) for block in range(blocks) for h in range(heads)]

    def save(index):
        block, h = items[index]
        copies = []
        for place, (low, high) in enumerate(chunk_list((block + 1) * rows)):
            part = pl.ds(low, high - low)
            copies.append(
                pltpu.make_async_copy(
                    exp_s.at[index % slots, part],
                    expon.at[h, block, part],
                    out_sem.at[index % slots, place],
                )
            )
        return copies

    for block in range(blocks):
        for copy in load(block):
            copy.start()
    tops = {}

    def score_step(index, low, high):
        block, h = items[index]
        scores = nt(key_s[low:high], query_s[h, block * rows : (block + 1) * rows])
        if high == (block + 1) * rows:
            key_place = lax.broadcasted_iota(jnp.int32, scores.shape, 0) + (low - block * rows)
            query_place = lax.broadcasted_iota(jnp.int32, scores.shape, 1)
            scores = jnp.where(key_place <= query_place, scores, -1e30)
        score_s[index % 2, low:high] = scores
        top = jnp.max(scores.reshape(-1, 8, rows), axis=0)
        tops[index] = jnp.maximum(tops[index], top) if index in tops else top

    def exp_step(index, low, high, top, carried):
        _, h = items[index]
        value = jnp.exp2(score_s[index % 2, low:high] - top)
        total = jnp.sum(value.reshape(-1, 8, rows), axis=0)
        value = value.astype(bf16)
        exp_s[index % slots, low:high] = value
        mixed = nn(v_t[h * size : (h + 1) * size, low:high], value)
        return (total, mixed) if carried is None else (carried[0] + total, carried[1] + mixed)

    for index in range(len(items) + 1):
        ahead, behind = [], []
        if index < len(items):
            block, h = items[index]
            if h == 0:
                for copy in load(block):
                    copy.wait()
            ahead = chunk_list((block + 1) * rows)
        if index:
            block, h = items[index - 1]
            behind = chunk_list((block + 1) * rows)
            top = jnp.max(tops[index - 1], axis=0, keepdims=True)
            carried = None
            if index - 1 >= slots:
                for copy in save(index - 1 - slots):
                    copy.wait()
        for place in range(max(len(ahead), len(behind))):
            if place < len(ahead):
                score_step(index, *ahead[place])
            if place < len(behind):
                carried = exp_step(index - 1, *behind[place], top, carried)
        if index:
            cols = slice(block_of(items, index - 1) * rows, (block_of(items, index - 1) + 1) * rows)
            inverse = 1.0 / jnp.sum(carried[0], axis=0, keepdims=True)
            inv_out[h : h + 1, cols] = inverse
            mixed = carried[1] * inverse
            full_t[h * size : (h + 1) * size, cols] = mixed
            mixed_s[h * size : (h + 1) * size, cols] = mixed.astype(bf16)
            for copy in save(index - 1):
                copy.start()
    for k_place in range(mp):
        target = lax.rem(me + k_place, mp)
        piece_refs[k_place][...] = mixed_s[:, pl.ds(pl.multiple_of(target * own, own), own)]
    for index in range(max(0, len(items) - slots), len(items)):
        for copy in save(index):
            copy.wait()


def block_of(items, index):
    return items[index][0]


def fwd_call(me, posq, slot, feature, k, v_t, mp, own):
    rows = BLOCK
    blocks = LEN // rows
    heads, _, model = posq.shape
    width = k.shape[1]
    slots = min(3, heads * blocks)
    anywhere = pl.BlockSpec(memory_space=pl.ANY)
    outs = [
        jax.ShapeDtypeStruct((heads, blocks, LEN, rows), bf16),
        jax.ShapeDtypeStruct((width, LEN), f32),
        jax.ShapeDtypeStruct((heads, LEN), f32),
    ] + [jax.ShapeDtypeStruct((width, own), bf16)] * mp
    return pl.pallas_call(
        functools.partial(fwd_kernel, mp, own),
        grid_spec=pltpu.PrefetchScalarGridSpec(
            num_scalar_prefetch=1,
            grid=(1,),
            in_specs=[anywhere] * 4 + [full(v_t.shape)],
            out_specs=[anywhere] + [full(o.shape) for o in outs[1:]],
            scratch_shapes=[
                pltpu.VMEM((LEN, model + width), bf16),
                pltpu.VMEM((heads, LEN, model + width), bf16),
                pltpu.VMEM((slots, LEN, rows), bf16),
                pltpu.VMEM((2, LEN, rows), f32),
                pltpu.VMEM((width, LEN), bf16),
                pltpu.SemaphoreType.DMA((blocks, 2 + 2 * heads)),
                pltpu.SemaphoreType.DMA((slots, -(-LEN // CHUNK))),
            ],
        ),
        out_shape=outs,
        compiler_params=params(),
        cost_estimate=pl.CostEstimate(
            flops=2 * heads * LEN * LEN * (model + 2 * width) * 6 // 10,
            bytes_accessed=20 << 20,
            transcendentals=heads * LEN * LEN * 6 // 10,
        ),
        name="attend",
    )(me, posq, slot, feature, k, v_t)


def bwd_kernel(mp, own, head, heads, score_scale, me_ref, *refs):
    g_refs = refs[:mp]
    (expon, full_t, inv, slot, feature_t, k_t, v, shift, w_pos_t, turn, turn_block, norm_all) = refs[mp : mp + 12]
    out = refs[mp + 12 :]
    piece_refs = out[:mp]
    dw_out, dpos, d_bias = out[mp : mp + 3]
    (grad_s, dk_s, dv_s, all_s, exp_s, key_s, v_s, slot_s, shift_s, full_s, norm_s, exp_sem, in_sem) = out[mp + 3 :]
    me = me_ref[0]
    _, blocks, _, rows = expon.shape
    size = full_s.shape[0]
    model = w_pos_t.shape[1]
    half = model // 2
    first_row = head * size

    def load_exp(block):
        copies = []
        for place, (low, high) in enumerate(chunk_list((block + 1) * rows)):
            part = pl.ds(low, high - low)
            copies.append(
                pltpu.make_async_copy(
                    expon.at[head, block, part], exp_s.at[block % 2, part], exp_sem.at[block % 2, place]
                )
            )
        return copies

    def load_block(block):
        cols = pl.ds(block * rows, rows)
        pairs = [
            (k_t.at[pl.ds(first_row, size), cols], key_s.at[pl.ds(0, size), cols]),
            (feature_t.at[:, cols], key_s.at[pl.ds(size, model), cols]),
            (v.at[cols], v_s.at[cols]),
            (slot.at[head, cols], slot_s.at[cols]),
            (shift.at[cols], shift_s.at[cols]),
            (full_t.at[pl.ds(first_row, size), cols], full_s.at[:, cols]),
        ]
        return [
            pltpu.make_async_copy(source, target, in_sem.at[block, place])
            for place, (source, target) in enumerate(pairs)
        ]

    norm_copy = pltpu.make_async_copy(norm_all, norm_s, in_sem.at[blocks, 0])
    for copy in load_exp(0) + load_block(0) + load_exp(1) + load_block(1):
        copy.start()
    for block in range(2, blocks):
        for copy in load_block(block):
            copy.start()
    norm_copy.start()
    for k in range(mp):
        source = lax.rem(me - k + mp, mp)
        grad_s[:, pl.ds(pl.multiple_of(source * own, own), own)] = g_refs[k][...]

    def masked_rows(part):
        if heads == 1:
            return part
        zeros = jnp.zeros((size, part.shape[1]), part.dtype)
        return jnp.concatenate([part if h == head else zeros for h in range(heads)], axis=0)

    d_content_sum = jnp.zeros((size, 1), f32)
    d_shift_sum = jnp.zeros((size, 1), f32)
    d_position = None
    for block in range(blocks):
        low, high = block * rows, (block + 1) * rows
        for copy in load_exp(block) + load_block(block):
            copy.wait()
        exp_b = exp_s.at[block % 2]
        grad = grad_s[:, low:high].astype(f32) * inv[head : head + 1, low:high]
        delta = jnp.sum(grad * full_s[:, low:high], axis=0, keepdims=True)
        grad = masked_rows(grad)
        grad_t = grad.astype(bf16)
        grad_n = grad.T.astype(bf16)
        queries = slot_s[low:high]
        joint = None
        chunks = chunk_list(high, rows)
        probs = {0: nn(v_s[chunks[0][0] : chunks[0][1]], grad_t)}
        for place, (start, end) in enumerate(chunks):
            if place + 1 < len(chunks):
                after = chunks[place + 1]
                probs[place + 1] = nn(v_s[after[0] : after[1]], grad_t)
            exp_c = exp_b[start:end]
            grad_scores = (exp_c.astype(f32) * (probs.pop(place) - delta)).astype(bf16)
            part = nn(key_s[:, start:end], grad_scores)
            joint = part if joint is None else joint + part
            d_value = nn(exp_c, grad_n)
            d_key = nn(grad_scores, queries)
            for part, target in ((d_value, dv_s), (d_key, dk_s)):
                old = max(0, min(end, low) - start)
                if old:
                    target[start : start + old] += part[:old]
                if old < end - start:
                    target[start + old : end] = part[old:]
        joint = joint * score_scale
        if block + 2 < blocks:
            for copy in load_exp(block + 2):
                copy.start()
        d_content, d_pos = joint[:size], joint[size:]
        g_cos, g_sin = d_pos[:half], d_pos[half:]
        sin_a, cos_a = turn_block[:, block : block + 1], turn_block[:, blocks + block : blocks + block + 1]
        sin_r, cos_r = turn[:half], turn[half:]
        sin = sin_a * cos_r + cos_a * sin_r
        cos = cos_a * cos_r - sin_a * sin_r
        d_coeff = jnp.concatenate(
            [
                (g_cos * sin - g_sin * cos).astype(bf16),
                (g_cos * cos + g_sin * sin).astype(bf16),
            ],
            axis=0,
        )
        part = nn(d_coeff, shift_s[low:high])
        if block:
            dpos[...] += part
        else:
            dpos[...] = part
        d_shift = nn(w_pos_t[...], d_coeff)
        d_content_sum = d_content_sum + jnp.sum(d_content, axis=1, keepdims=True)
        d_shift_sum = d_shift_sum + jnp.sum(d_shift, axis=1, keepdims=True)
        all_s[:size, low:high] = (d_content + d_shift).astype(bf16)

    mine = slice(first_row, first_row + size)
    all_s[size : 2 * size] = (dk_s[...] * (1.0 / log2_e)).T[mine].astype(bf16)
    all_s[2 * size :] = dv_s[...].T[mine].astype(bf16)
    for k in range(mp):
        target = lax.rem(me + k, mp)
        piece_refs[k][...] = all_s[:, pl.ds(pl.multiple_of(target * own, own), own)]
    both = jnp.concatenate([d_content_sum, d_shift_sum], axis=0)
    d_bias[...] = jnp.broadcast_to(both, (2 * size, 128)).T[:8]
    norm_copy.wait()
    dw_out[...] = nn(all_s[...], norm_s[...]).astype(bf16)


def bwd_call(
    me, head, heads, pieces, expon, full_t, inv, slot, feature_t, k_t, v, shift, w_pos_t, turns_t, norm_all, scale
):
    mp = len(pieces)
    size, own = pieces[0].shape
    _, blocks, _, rows = expon.shape
    width = v.shape[1]
    model = norm_all.shape[1]
    anywhere = pl.BlockSpec(memory_space=pl.ANY)
    turn, turn_block = turns_t
    return pl.pallas_call(
        functools.partial(bwd_kernel, mp, own, head, heads, scale),
        grid_spec=pltpu.PrefetchScalarGridSpec(
            num_scalar_prefetch=1,
            grid=(1,),
            in_specs=[full((size, own))] * mp
            + [anywhere, anywhere, full(inv.shape), anywhere, anywhere, anywhere, anywhere, anywhere]
            + [
                pl.BlockSpec((size, model), lambda i, m: (head, 0)),
                full(turn.shape),
                full(turn_block.shape),
                anywhere,
            ],
            out_specs=[full((3 * size, own))] * mp
            + [full((3 * size, model)), full((model, width)), full((8, 2 * size))],
            scratch_shapes=[
                pltpu.VMEM((size, LEN), bf16),
                pltpu.VMEM((LEN, width), f32),
                pltpu.VMEM((LEN, width), f32),
                pltpu.VMEM((3 * size, LEN), bf16),
                pltpu.VMEM((2, LEN, rows), bf16),
                pltpu.VMEM((size + model, LEN), bf16),
                pltpu.VMEM((LEN, width), bf16),
                pltpu.VMEM((LEN, width), bf16),
                pltpu.VMEM((LEN, width), bf16),
                pltpu.VMEM((size, LEN), f32),
                pltpu.VMEM((LEN, model), bf16),
                pltpu.SemaphoreType.DMA((2, -(-LEN // CHUNK))),
                pltpu.SemaphoreType.DMA((blocks + 1, 6)),
            ],
        ),
        out_shape=[jax.ShapeDtypeStruct((3 * size, own), bf16)] * mp
        + [
            jax.ShapeDtypeStruct((3 * size, model), bf16),
            jax.ShapeDtypeStruct((model, width), f32),
            jax.ShapeDtypeStruct((8, 2 * size), f32),
        ],
        compiler_params=params(),
        cost_estimate=pl.CostEstimate(
            flops=2 * LEN * LEN * (model + 4 * width) * 6 // 10, bytes_accessed=24 << 20, transcendentals=0
        ),
        name="attend_back",
    )(me, *pieces, expon, full_t, inv, slot, feature_t, k_t, v, shift, w_pos_t, turn, turn_block, norm_all)


KINDS = ("up", "down", "pred", "out")


def rows_kernel(mp, heads, dp, me_ref, *refs):
    count = heads * mp
    sources = 1 if dp else 4
    pieces, id_parts = refs[:mp], refs[mp : 2 * mp]
    refs = refs[2 * mp :]
    (labels, cotangent, table, vecs, logit_bias), refs = refs[:5], refs[5:]
    own_weights, gathered, out = refs[:4], refs[4 : 4 + sources], refs[4 + sources :]
    back = out[:count]
    block_out, grad_mid, d_vec, d_norm, d_scalar = out[count : count + 5]
    d_weights, out = out[count + 5 : count + 5 + sources], out[count + 5 + sources :]
    weights, stages, out = out[:4], out[4:8], out[8:]
    (norm_mid_s, norm_mid_t, hidden, slope, p_hidden, p_slope, cot_s, grads, in_sem, out_sem) = out
    gain, bias, down_bias = vecs[2:3], vecs[3:4], vecs[4:5]
    me = me_ref[0]
    width = pieces[0].shape[0]
    size = width // heads
    own, model = block_out.shape

    def row_range(kind):
        row = sum(ref.shape[2] for ref in weights[:kind])
        return pl.ds(row, weights[kind].shape[2])

    def load(kind, c):
        if c == 0:
            source = own_weights[kind]
        elif dp:
            source = gathered[0].at[:, c - 1, row_range(kind)]
        else:
            source = gathered[kind].at[c - 1]
        return pltpu.make_async_copy(source, weights[kind].at[c], in_sem.at[kind, c])

    def weight(name, c):
        kind = KINDS.index(name)
        load(kind, c).wait()
        return again(name, c)

    def again(name, c):
        ref = weights[KINDS.index(name)]
        return ref[c].reshape(-1, ref.shape[-1])

    def store(name, c, value):
        kind = KINDS.index(name)
        stages[kind][c] = value.astype(bf16).reshape(stages[kind].shape[1:])
        copy = out_copy(kind, c)
        copy.start()

    def out_copy(kind, c):
        place = lax.rem(me - c + mp, mp)
        target = d_weights[0].at[:, place, row_range(kind)] if dp else d_weights[kind].at[place]
        return pltpu.make_async_copy(stages[kind].at[c], target, out_sem.at[kind, c])

    cot_copy = pltpu.make_async_copy(cotangent, cot_s, in_sem.at[4, 0])
    for c in range(mp):
        load(3, c).start()
    for c in range(mp):
        load(0, c).start()
        load(1, c).start()
    for c in range(mp):
        load(2, c).start()
    cot_copy.start()

    vec = [ref[1:4].astype(f32) for ref in id_parts]
    _, middle = embed_rows(id_parts[0][0:1], table[...])
    for k in range(mp):
        part = pieces[k][...].astype(f32).T.astype(bf16)
        middle = middle + nn(part, weight("out", k))
    xhat, inverse = layer_stats(middle)
    mid = xhat * gain + bias
    norm_mid_s[...] = mid.astype(bf16)
    norm_mid_t[...] = mid.T.astype(bf16)

    halves = [slice(low, low + own // 2) for low in (0, own // 2)]
    items = [(c, h) for c in range(mp) for h in range(2)]
    last = len(items) - 1
    total = [middle[rows] + down_bias for rows in halves]
    first = {}

    def up_ahead(index):
        c, h = items[index]
        matrix = weight("up", c) if h == 0 else again("up", c)
        first[index] = nn(norm_mid_s[halves[h]], matrix)

    def down_behind(index):
        c, h = items[index]
        matrix = weight("down", c) if h == 0 else again("down", c)
        total[h] = total[h] + nn(hidden[c, halves[h]], matrix)

    up_ahead(0)
    for index, (c, h) in enumerate(items):
        if index < last:
            up_ahead(index + 1)
        value, grad = gelu_parts(first.pop(index) + vec[c][0:1])
        hidden[c, halves[h]] = value.astype(bf16)
        slope[c, halves[h]] = grad
        if index:
            down_behind(index - 1)
    down_behind(last)

    for h, rows in enumerate(halves):
        block_out[rows] = total[h].astype(bf16)
    out_low_t = block_out[...].astype(f32).T.astype(bf16)
    logits = [jnp.zeros((own // 2, 1), f32) for _ in halves]

    def pred_ahead(index):
        c, h = items[index]
        matrix = weight("pred", c) if h == 0 else again("pred", c)
        first[index] = nn(block_out[halves[h]], matrix)

    pred_ahead(0)
    for index, (c, h) in enumerate(items):
        if index < last:
            pred_ahead(index + 1)
        value, grad = gelu_parts(first.pop(index) + vec[c][1:2])
        value = value.astype(bf16)
        p_hidden[c, halves[h]] = value
        p_slope[c, halves[h]] = grad
        logits[h] = logits[h] + jnp.sum(value.astype(f32) * vec[c][2:3], axis=1, keepdims=True)

    label = jnp.broadcast_to(labels[0], (128, own)).T[:, :1]
    x = jnp.concatenate(logits, axis=0) + logit_bias[...]
    fall = jnp.exp(-jnp.abs(x))
    loss = jnp.maximum(x, 0.0) + jnp.log(1.0 + fall) - label * x
    grad = jnp.where(x >= 0, 1.0, fall) / (1.0 + fall) - label
    d_scalar[0:1] = jnp.broadcast_to(jnp.sum(loss, axis=0, keepdims=True), (1, 128))
    d_scalar[1:2] = jnp.broadcast_to(jnp.sum(grad, axis=0, keepdims=True), (1, 128))
    g_logit = grad.astype(bf16).astype(f32)

    cot_copy.wait()
    total = [cot_s[rows].astype(f32) for rows in halves]

    def pred_behind(index):
        c, h = items[index]
        total[h] = total[h] + nt(grads[c % 2, halves[h]], again("pred", c))
        if h == 1:
            store("pred", c, nn(out_low_t, grads[c % 2]))

    sums = {}

    def add_sum(key, value):
        value = jnp.sum(value, axis=0, keepdims=True)
        sums[key] = sums[key] + value if key in sums else value

    for index, (c, h) in enumerate(items):
        rows = halves[h]
        g_pre = g_logit[rows] * vec[c][2:3] * p_slope[c, rows]
        add_sum((c, 1), g_pre)
        add_sum((c, 2), g_logit[rows] * p_hidden[c, rows].astype(f32))
        grads[c % 2, rows] = g_pre.astype(bf16)
        if index:
            pred_behind(index - 1)
    pred_behind(last)

    d_norm[2:3] = sum(jnp.sum(part, axis=0, keepdims=True) for part in total)
    grad_out = total
    for h, rows in enumerate(halves):
        cot_s[rows] = grad_out[h].astype(bf16)
    total = [jnp.zeros((own // 2, model), f32) for _ in halves]

    def back_ahead(index):
        c, h = items[index]
        first[index] = nt(cot_s[halves[h]], again("down", c))

    def up_behind(index):
        c, h = items[index]
        total[h] = total[h] + nt(grads[c % 2, halves[h]], again("up", c))
        if h == 1:
            store("up", c, nn(norm_mid_t[...], grads[c % 2]))

    back_ahead(0)
    for index, (c, h) in enumerate(items):
        rows = halves[h]
        if index < last:
            back_ahead(index + 1)
        g_up = first.pop(index) * slope[c, rows]
        add_sum((c, 0), g_up)
        grads[c % 2, rows] = g_up.astype(bf16)
        if index:
            up_behind(index - 1)
        if h == 0:
            store("down", c, tn(hidden[c], cot_s[...]))
    up_behind(last)
    for (c, kind), value in sums.items():
        d_vec[lax.rem(me - c + mp, mp), kind : kind + 1] = value
    total = jnp.concatenate(total, axis=0)
    grad_out = jnp.concatenate(grad_out, axis=0)

    d_norm[0:1] = jnp.sum(total * xhat, axis=0, keepdims=True)
    d_norm[1:2] = jnp.sum(total, axis=0, keepdims=True)
    g_mid = grad_out + norm_back(total, xhat, inverse, gain)
    g_low = g_mid.astype(bf16)
    for k in range(mp):
        part = nt(again("out", (mp - k) % mp), g_low).astype(bf16)
        for h in range(heads):
            back[h * mp + k][...] = part[h * size : (h + 1) * size]
    grad_mid[...] = g_mid
    for k in range(mp):
        store("out", k, nn(pieces[k][...], g_low))
    for kind in range(4):
        for c in range(mp):
            out_copy(kind, c).wait()


def rows_call(me, pieces, heads, id_parts, labels, cotangent, table, vecs, logit_bias, own_weights, weights, dp):
    mp = len(id_parts)
    width, own = pieces[0].shape
    size = width // heads
    model = table.shape[1]
    hid = own_weights[0].shape[1]
    outs = [jax.ShapeDtypeStruct((size, own), bf16)] * (heads * mp) + [
        jax.ShapeDtypeStruct((own, model), bf16),
        jax.ShapeDtypeStruct((own, model), f32),
        jax.ShapeDtypeStruct((mp, 3, hid), f32),
        jax.ShapeDtypeStruct((3, model), f32),
        jax.ShapeDtypeStruct((2, 128), f32),
    ]
    out_specs = [full(o.shape) for o in outs]
    anywhere = pl.BlockSpec(memory_space=pl.ANY)
    if dp:
        own_weights = [w.reshape(dp, -1, model) for w in own_weights]
        weights = [weights]
        rows = sum(w.shape[1] for w in own_weights)
        outs.append(jax.ShapeDtypeStruct((dp, mp, rows, model), bf16))
        out_specs.append(anywhere)
    else:
        own_weights = [w[None] for w in own_weights]
        weights = [w[:, None] for w in weights]
        for w in own_weights:
            outs.append(jax.ShapeDtypeStruct((mp, *w.shape), bf16))
            out_specs.append(anywhere)
    held = [pltpu.VMEM((mp, *w.shape), bf16) for w in own_weights]
    ins = [*pieces, *id_parts]
    rest = [table, vecs, logit_bias]
    return pl.pallas_call(
        functools.partial(rows_kernel, mp, heads, dp),
        grid_spec=pltpu.PrefetchScalarGridSpec(
            num_scalar_prefetch=1,
            grid=(1,),
            in_specs=[full(a.shape) for a in ins]
            + [pl.BlockSpec((1, 1, own), lambda s, m: (m[0], 0, 0)), anywhere]
            + [full(a.shape) for a in rest]
            + [anywhere] * (4 + len(weights)),
            out_specs=out_specs,
            scratch_shapes=held
            + held
            + [
                pltpu.VMEM((own, model), bf16),
                pltpu.VMEM((model, own), bf16),
                pltpu.VMEM((mp, own, hid), bf16),
                pltpu.VMEM((mp, own, hid), f32),
                pltpu.VMEM((mp, own, hid), bf16),
                pltpu.VMEM((mp, own, hid), f32),
                pltpu.VMEM((own, model), bf16),
                pltpu.VMEM((2, own, hid), bf16),
                pltpu.SemaphoreType.DMA((5, mp)),
                pltpu.SemaphoreType.DMA((4, mp)),
            ],
        ),
        out_shape=outs,
        compiler_params=params(),
        cost_estimate=pl.CostEstimate(
            flops=18 * own * model * hid * mp, bytes_accessed=20 << 20, transcendentals=2 * own * hid * mp
        ),
        name="rows",
    )(me, *ins, labels, cotangent, *rest, *own_weights, *weights)


SIDE = 64
VEC_ROWS = 24


def packed(value, model):
    side = value[:, model : model + SIDE] + value[:, model + SIDE :]
    high = side.astype(bf16)
    low = (side - high.astype(f32)).astype(bf16)
    return jnp.concatenate([value[:, :model].astype(bf16), high, low], axis=1)


def tail_kernel(mp, heads, split, me_ref, *refs):
    count = heads * mp
    pieces = refs[:count]
    own_joint, joint_rest, ids, table, vecs, grad_mid = refs[count : count + 6]
    refs = refs[count + 6 :]
    if split:
        d_norm_two, d_vec, d_scalar = refs[:3]
        d_biases = refs[3 : 3 + heads]
        grad_in, sent, parts, vec_s, sums = refs[3 + heads :]
    else:
        grad_in, d_embed, d_norm, parts = refs
    me = me_ref[0]
    size = pieces[0].shape[0] // 3
    width = heads * size
    for h in range(heads):
        for k in range(mp):
            for kind in range(3):
                row = (k * 3 + kind) * width + h * size
                parts[row : row + size] = pieces[h * mp + k][kind * size : (kind + 1) * size]
    g_norm = tn(parts[: 3 * width], own_joint[...])
    for k in range(1, mp):
        part = parts[k * 3 * width : (k + 1) * 3 * width]
        g_norm = g_norm + tn(part, joint_rest[:, k - 1].reshape(3 * width, -1))
    one_hot_t, inputs = embed_rows(ids[0:1], table[...])
    normed, inverse = layer_stats(inputs)
    d_gain = jnp.sum(g_norm * normed, axis=0, keepdims=True)
    d_bias = jnp.sum(g_norm, axis=0, keepdims=True)
    g_in = grad_mid[...] + norm_back(g_norm, normed, inverse, vecs[0:1])
    first = g_in.astype(bf16)
    grad_in[...] = first
    rest = g_in - first.astype(f32)
    second = rest.astype(bf16)
    third = (rest - second.astype(f32)).astype(bf16)
    hot = one_hot_t.astype(bf16)
    embed = nn(hot, first) + nn(hot, second) + nn(hot, third)
    if not split:
        d_embed[...] = embed
        d_norm[0:1] = d_gain
        d_norm[1:2] = d_bias
        return
    model = grad_mid.shape[1]
    vec_s[...] = jnp.zeros_like(vec_s)
    vec_s[0:1] = d_gain
    vec_s[1:2] = d_bias
    vec_s[2:5] = d_norm_two[...]
    for z in range(mp):
        vec_s[5 + 3 * z : 8 + 3 * z] = d_vec[z]
    sums[:, :model] = embed
    sums[:, model:] = jnp.zeros((sums.shape[0], 2 * SIDE), f32)
    for g in range(model // SIDE):
        sums[g * VEC_ROWS : (g + 1) * VEC_ROWS, model : model + SIDE] = vec_s[
            :, g * SIDE : (g + 1) * SIDE
        ]
    start = VEC_ROWS * (model // SIDE)
    for z in range(mp):
        for h in range(heads):
            row = start + 8 * z + 2 * h
            for kind in range(2):
                values = d_biases[h][0:1, kind * size : (kind + 1) * size]
                sums[row + kind : row + kind + 1, model : model + SIDE] = jnp.where(me == z, values, 0.0)
    row = start + 8 * mp
    sums[row : row + 2, model : model + SIDE] = d_scalar[:, :SIDE]
    sent[...] = packed(sums[...], model).reshape(sent.shape)


def tail_call(me, pieces, heads, own_joint, joint_rest, ids, table, vecs, grad_mid, smalls, dp):
    mp = len(pieces) // heads
    own, model = grad_mid.shape
    vocab = table.shape[0]
    wide = model + 2 * SIDE
    outs = [jax.ShapeDtypeStruct((own, model), bf16)]
    scratch = [pltpu.VMEM((mp * own_joint.shape[0], own), bf16)]
    if smalls:
        outs.append(jax.ShapeDtypeStruct((dp, vocab // dp, wide), bf16))
        scratch += [pltpu.VMEM((VEC_ROWS, model), f32), pltpu.VMEM((vocab, wide), f32)]
    else:
        outs += [jax.ShapeDtypeStruct(table.shape, f32), jax.ShapeDtypeStruct((2, model), f32)]
    ins = [*pieces, own_joint, joint_rest, ids, table, vecs, grad_mid, *smalls]
    return grid_call(
        functools.partial(tail_kernel, mp, heads, bool(smalls)), "tail", me, ins, outs, scratch
    )


def grid_call(kernel, name, me, ins, outs, scratch=()):
    return pl.pallas_call(
        kernel,
        grid_spec=pltpu.PrefetchScalarGridSpec(
            num_scalar_prefetch=1,
            grid=(1,),
            in_specs=[full(a.shape) for a in ins],
            out_specs=[full(o.shape) for o in outs],
            scratch_shapes=list(scratch),
        ),
        out_shape=outs,
        compiler_params=params(),
        cost_estimate=pl.CostEstimate(
            flops=1 << 28,
            bytes_accessed=sum(math.prod(a.shape) * a.dtype.itemsize for a in [*ins, *outs]),
            transcendentals=0,
        ),
        name=name,
    )(me, *ins)


def whole_call(kernel, name, me, ins, outs, scratch=()):
    vmem = pl.BlockSpec(memory_space=pltpu.VMEM)
    return pl.pallas_call(
        kernel,
        in_specs=[pl.BlockSpec(memory_space=pltpu.SMEM)] + [vmem] * len(ins),
        out_specs=[vmem] * len(outs),
        out_shape=outs,
        scratch_shapes=list(scratch),
        compiler_params=pltpu.CompilerParams(vmem_limit_bytes=SMALL_VMEM_BYTES),
        cost_estimate=pl.CostEstimate(
            flops=1 << 20,
            bytes_accessed=sum(math.prod(a.shape) * a.dtype.itemsize for a in [*ins, *outs]),
            transcendentals=0,
        ),
        name=name,
    )(me, *ins)


def shift_pairs(count, k):
    return [(s, (s + k) % count) for s in range(count)]


def exchange(parts, axis, count):
    return [parts[0]] + [
        lax.ppermute(parts[k], axis, shift_pairs(count, k)) for k in range(1, count)
    ]


def add_parts(parts):
    value = parts[0].astype(f32)
    for place in range(1, parts.shape[0]):
        value = value + parts[place].astype(f32)
    return value


def plane_kernel(model, me_ref, parts, out):
    out[...] = packed(add_parts(parts), model)


def line_kernel(mp, model, me_ref, *refs):
    parts, out, held = refs[:mp], refs[mp], refs[mp + 1]
    me = me_ref[0]
    for k in range(mp):
        held[lax.rem(me - k + mp, mp)] = parts[k][...]
    value = packed(add_parts(held), model)
    for place in range(out.shape[0]):
        out[place] = value


def small_kernel(mp, heads, size, scale, me_ref, parts, *refs):
    d_embed, gain1, bias1, gain2, bias2, down, up_b, pred_b, logit_w, cb, pb, loss, logit_b, vec_s = refs
    model = d_embed.shape[1]
    held = parts[...].reshape(-1, parts.shape[2])
    d_embed[...] = held[:, :model].astype(f32)
    side = held[:, model:].astype(f32)
    side = side[:, :SIDE] + side[:, SIDE:]
    for g in range(model // SIDE):
        vec_s[:, g * SIDE : (g + 1) * SIDE] = side[g * VEC_ROWS : (g + 1) * VEC_ROWS]
    for place, ref in enumerate((gain1, bias1, gain2, bias2, down)):
        ref[...] = vec_s[place : place + 1]
    me = me_ref[0]
    start = VEC_ROWS * (model // SIDE)
    for place, ref in enumerate((up_b, pred_b, logit_w)):
        value = vec_s[5 + place : 6 + place]
        for z in range(1, mp):
            value = jnp.where(me == z, vec_s[5 + 3 * z + place : 6 + 3 * z + place], value)
        ref[...] = value
    for h in range(heads):
        for kind, ref in enumerate((cb, pb)):
            row = start + 2 * h + kind
            value = side[row : row + 1]
            for z in range(1, mp):
                value = jnp.where(me == z, side[row + 8 * z : row + 8 * z + 1], value)
            ref[h : h + 1] = value[:, :size]
    row = start + 8 * mp
    loss[...] = side[row : row + 1, :1] * scale
    logit_b[...] = side[row + 1 : row + 2, :1]


def heads_kernel(heads, me_ref, *refs):
    joints, poses = refs[:heads], refs[heads : 2 * heads]
    out, joint, pos = refs[2 * heads :]
    size = joints[0].shape[0] // 3
    width = heads * size
    for h in range(heads):
        for kind in range(3):
            row = kind * width + h * size
            joint[row : row + size] = joints[h][kind * size : (kind + 1) * size]
    value = poses[0][...]
    lane = lax.broadcasted_iota(jnp.int32, value.shape, 1)
    for h in range(1, heads):
        value = jnp.where(lane >= h * size, poses[h][...], value)
    pos[...] = value.astype(bf16)
    pieces = out.shape[0]
    groups = joint.shape[1] // width
    j_rows = joint.shape[0] // pieces
    p_rows = pos.shape[0] // pieces // groups
    for piece in range(pieces):
        out[piece, :j_rows] = joint[piece * j_rows : (piece + 1) * j_rows]
        start = piece * p_rows * groups
        for g in range(groups):
            out[piece, j_rows:, g * width : (g + 1) * width] = pos[
                start + g * p_rows : start + (g + 1) * p_rows
            ]


def lines_kernel(mp, me_ref, part, *outs):
    for k in range(mp):
        outs[k][...] = part[lax.rem(me_ref[0] + k, mp)]


def merge_kernel(mp, me_ref, *refs):
    lines, by_heads, out = refs[:mp], refs[mp], refs[mp + 1]
    value = lines[0][...].astype(f32)
    for k in range(1, mp):
        value = value + lines[k][...].astype(f32)
    rows = value.shape[0]
    out[:rows] = value.astype(bf16)
    out[rows:] = add_parts(by_heads).astype(bf16)


def spread_kernel(order, me_ref, *refs):
    dp = len(order)
    parts = refs[:dp]
    up, down, pred, out, query, key, value, pos, joint = refs[dp:]
    width = pos.shape[1]
    groups = joint.shape[1] // width
    for bits, part in zip(order, parts):
        source = jnp.bitwise_xor(me_ref[1], bits)
        row = 0
        for ref in (up, down, pred, out, joint):
            rows = ref.shape[0] // dp
            place = pl.multiple_of(source * rows, rows)
            ref[pl.ds(place, rows)] = part[row : row + rows].astype(f32)
            row += rows
        rows = pos.shape[0] // dp // groups
        for g in range(groups):
            place = pl.multiple_of((source * groups + g) * rows, rows)
            pos[pl.ds(place, rows)] = part[row : row + rows, g * width : (g + 1) * width].astype(f32)
    for kind, ref in enumerate((query, key, value)):
        ref[...] = joint[kind * width : (kind + 1) * width].T


def swap(value, dp, bits):
    return lax.ppermute(value, "dp", [(s, s ^ bits) for s in range(dp)])


def trade(parts, axis):
    return lax.all_to_all(parts, axis, 0, 0)


def sum_heads(me, joints, poses, dp):
    model = joints[0].shape[1]
    width = poses[0].shape[1]
    (parts,) = grid_call(
        functools.partial(heads_kernel, len(joints)),
        "cut_heads",
        me,
        [*joints, *poses],
        [jax.ShapeDtypeStruct((dp, 4 * width // dp, model), bf16)],
        [pltpu.VMEM((3 * width, model), bf16), pltpu.VMEM((model, width), bf16)],
    )
    return trade(parts, "dp")


def sum_all(me, grads, by_heads, sent, dp, mp, heads, size):
    model = grads.shape[-1]
    width = heads * size
    summed = lax.psum_scatter(grads, "dp", scatter_dimension=0, tiled=True).reshape(mp, -1, model)
    summed, by_heads = lax.optimization_barrier((summed, by_heads))
    rows = summed.shape[1]
    line = [jax.ShapeDtypeStruct((rows, model), bf16)] * mp
    line = whole_call(functools.partial(lines_kernel, mp), "cut_lines", me, [summed], line)
    line = exchange(line, "mp", mp)
    got = trade(sent, "dp")
    got, *line = lax.optimization_barrier((got, *line))
    piece = jax.ShapeDtypeStruct(got.shape[1:], bf16)
    (part,) = whole_call(functools.partial(plane_kernel, model), "add_plane", me, [got], [piece])
    (weight_part,) = whole_call(
        functools.partial(merge_kernel, mp),
        "merge",
        me,
        [*line, by_heads],
        [jax.ShapeDtypeStruct((rows + by_heads.shape[1], model), bf16)],
    )
    got = exchange([part] * mp, "mp", mp)
    order, weight_parts = [], []
    for bits in range(0, dp, 2):
        there = swap(weight_part, dp, bits) if bits else weight_part
        order += [bits, bits + 1]
        weight_parts += [there, swap(there, dp, 1)]
    (part,) = whole_call(
        functools.partial(line_kernel, mp, model),
        "add_line",
        me,
        got,
        [jax.ShapeDtypeStruct((dp, *piece.shape), bf16)],
        [pltpu.VMEM((mp, *piece.shape), bf16)],
    )
    got = trade(part, "dp")
    row = jax.ShapeDtypeStruct((1, model), f32)
    one = jax.ShapeDtypeStruct((1, 1), f32)
    by_head = jax.ShapeDtypeStruct((heads, size), f32)
    outs = [jax.ShapeDtypeStruct((dp * piece.shape[0], model), f32)] + [row] * 8 + [by_head] * 2 + [one] * 2
    small = whole_call(
        functools.partial(small_kernel, mp, heads, size, 1.0 / (LEN * dp)),
        "small_sums",
        me,
        [got],
        outs,
        [pltpu.VMEM((VEC_ROWS, model), f32)],
    )
    square = jax.ShapeDtypeStruct((model, model), f32)
    thin = jax.ShapeDtypeStruct((model, width), f32)
    outs = [square] * 3 + [jax.ShapeDtypeStruct((width, model), f32)] + [thin] * 4
    weights = whole_call(
        functools.partial(spread_kernel, order),
        "spread",
        me,
        weight_parts,
        outs,
        [pltpu.VMEM((3 * width, model), f32)],
    )
    return weights, small


def per_device(
    byte_ids,
    embed_table,
    boundary_labels,
    out_cotangent,
    norm_one_gain,
    norm_one_bias,
    w_query,
    w_key,
    w_value,
    w_position,
    content_bias,
    position_bias,
    w_out,
    norm_two_gain,
    norm_two_bias,
    w_up,
    up_bias,
    w_down,
    down_bias,
    w_pred,
    pred_bias,
    w_logit,
    logit_bias,
):
    dp, mp = lax.axis_size("dp"), lax.axis_size("mp")
    me_dp, me_mp = lax.axis_index("dp"), lax.axis_index("mp")
    own = byte_ids.shape[0]
    assert boundary_labels.shape[0] == LEN and own * mp == LEN and w_up.shape[1] == own
    model = embed_table.shape[1]
    vocab = embed_table.shape[0]
    heads, size = content_bias.shape
    width = heads * size
    hid = w_up.shape[1]
    scale = 1.0 / math.sqrt(size)
    planned = (
        hid == model
        and size == SIDE
        and dp & (dp - 1) == 0
        and width % (16 * dp) == 0
        and vocab % (16 * dp) == 0
        and VEC_ROWS * (model // SIDE) + 8 * mp + 2 <= vocab
        and 5 + 3 * mp <= VEC_ROWS
        and 2 * heads <= 8
    )
    me = jnp.stack([me_mp, me_dp]).astype(jnp.int32)
    own_weights = (w_up, w_down, w_pred, w_out)
    shorts = [byte_ids, up_bias, pred_bias, w_logit, norm_one_gain, norm_one_bias, norm_two_gain, norm_two_bias]
    shorts += [down_bias, content_bias, position_bias, logit_bias, boundary_labels]
    shorts += [w_query, w_key, w_value, w_position]
    prepared = prep_call(me, shorts, own_weights, mp, dp if planned else 0)
    head_rows, vecs, biases, labels, logit_row, w_joint, w_pos_t, joint_t = prepared[:8]

    id_parts = exchange([head_rows] * mp, "mp", mp)

    if planned:
        *id_parts, shares = lax.optimization_barrier((*id_parts, prepared[8]))
        shares = exchange([shares] * mp, "mp", mp)[1:]
    else:
        weights = [jnp.stack(exchange([w] * mp, "mp", mp)[1:]) for w in own_weights]
        joint_rest = jnp.stack(exchange([joint_t] * mp, "mp", mp)[1:])[None]

    feature, turn, turn_block = feature_tables(model)
    turns = (jnp.asarray(turn), jnp.asarray(turn_block))
    turns_t = (
        jnp.asarray(np.ascontiguousarray(turn.T)),
        jnp.asarray(np.ascontiguousarray(turn_block.reshape(2, -1, model // 2).transpose(2, 0, 1).reshape(model // 2, -1))),
    )
    feature_t = jnp.asarray(np.ascontiguousarray(feature.T))
    feature = jnp.asarray(feature)

    norm_all, posq, slot, k, k_t, v, v_t, shift = pre_call(
        me,
        id_parts,
        embed_table,
        vecs,
        w_joint,
        w_position,
        biases,
        turns,
        heads,
        scale,
    )
    if planned:
        posq, *shares = lax.optimization_barrier((posq, *shares))
        shares = jnp.stack(shares)
        cut = shares.shape[1] - 3 * width // dp
        weights = lax.all_gather(shares[:, :cut], "dp", axis=0, tiled=False)
    expon, full_t, inv, *sent = fwd_call(me, posq, slot, feature, k, v_t, mp, own)
    sent = exchange(sent, "mp", mp)

    if planned:
        *sent, joint_rest = lax.optimization_barrier((*sent, shares[:, cut:]))
        joint_rest = lax.all_gather(joint_rest, "dp", axis=0, tiled=False)
    result = rows_call(
        me,
        sent,
        heads,
        id_parts,
        labels,
        out_cotangent,
        embed_table,
        vecs,
        logit_row,
        own_weights,
        weights,
        dp if planned else 0,
    )
    back = result[: heads * mp]
    block_out, grad_mid, d_vec, d_norm_two, d_scalar, *d_weights = result[heads * mp :]

    if planned:
        d_weights[0], joint_rest = lax.optimization_barrier((d_weights[0], joint_rest))
    arrived, d_joint, d_pos, d_bias = [], [], [], []
    for h in range(heads):
        pieces = exchange(back[h * mp : (h + 1) * mp], "mp", mp)
        if h:
            slot, _ = lax.optimization_barrier((slot, parts[0]))
        parts = bwd_call(
            me,
            h,
            heads,
            pieces,
            expon,
            full_t,
            inv,
            slot,
            feature_t,
            k_t,
            v,
            shift,
            w_pos_t,
            turns_t,
            norm_all,
            scale,
        )
        if h:
            parts = lax.optimization_barrier((*parts, *arrived[1:]))[: len(parts)]
        arrived += exchange(parts[:mp], "mp", mp)
        d_joint.append(parts[mp])
        d_pos.append(parts[mp + 1])
        d_bias.append(parts[mp + 2])
    smalls = [d_norm_two, d_vec, d_scalar, *d_bias] if planned else []
    if planned:
        by_heads = sum_heads(me, d_joint, d_pos, dp)
        *arrived, by_heads = lax.optimization_barrier((*arrived, by_heads))
    grad_input, *rest = tail_call(
        me, arrived, heads, joint_t, joint_rest, head_rows, embed_table, vecs, grad_mid, smalls, dp
    )

    if planned:
        weight_sums, small = sum_all(me, d_weights[0], by_heads, *rest, dp, mp, heads, size)
        up, down, pred, out, query, key, value, pos = weight_sums
        embed, gain1, bias1, gain2, bias2, down_b, up_b, pred_b, logit_w, cb, pb, loss, logit_b = small
    else:
        d_embed, d_norm_one = rest

        def shard_sum(value):
            summed = lax.psum(value, ("dp", "mp"))
            return lax.dynamic_index_in_dim(summed, me_mp, 0, keepdims=False).astype(f32)

        up, down, pred, out = [shard_sum(g[:, 0]) for g in d_weights]
        up_b, pred_b, logit_w = shard_sum(d_vec)
        joint = lax.psum(jnp.stack(d_joint), "dp").astype(f32)
        joint = joint.reshape(heads, 3, size, model).transpose(1, 3, 0, 2).reshape(3, model, width)
        query, key, value = joint
        pos = jnp.concatenate(
            [d_pos[h][:, h * size : (h + 1) * size] for h in range(heads)], axis=1
        )
        pos = lax.psum(pos.astype(bf16), "dp").astype(f32)
        biases = lax.psum(jnp.stack([d[0] for d in d_bias]), "dp")
        cb, pb = biases[:, :size], biases[:, size:]
        embed, norm_one, norm_two, scalars = lax.psum(
            (d_embed, d_norm_one, d_norm_two, d_scalar), ("dp", "mp")
        )
        gain1, bias1 = norm_one
        gain2, bias2, down_b = norm_two
        loss = scalars[0, :1] / (LEN * dp)
        logit_b = scalars[1, :1]
    flat = lambda v: v.reshape(-1)
    return (
        block_out,
        flat(loss),
        grad_input,
        embed,
        flat(gain1),
        flat(bias1),
        query,
        key,
        value,
        pos,
        cb,
        pb,
        out,
        flat(gain2),
        flat(bias2),
        up,
        flat(up_b),
        down,
        flat(down_b),
        pred,
        flat(pred_b),
        flat(logit_w),
        flat(logit_b),
    )


def solution(mesh):
    by_rows = P(("dp", "mp"), None)
    columns = P(None, "mp")
    shard = P("mp", None)
    placed = (
        P(("dp", "mp")),
        P(),
        P("dp"),
        by_rows,
        P(),
        P(),
        columns,
        columns,
        columns,
        columns,
        shard,
        shard,
        shard,
        P(),
        P(),
        columns,
        P("mp"),
        shard,
        P(),
        columns,
        P("mp"),
        P("mp"),
        P(),
    )
    results = (
        by_rows,
        P(),
        by_rows,
        P(),
        P(),
        P(),
        columns,
        columns,
        columns,
        columns,
        shard,
        shard,
        shard,
        P(),
        P(),
        columns,
        P("mp"),
        shard,
        P(),
        columns,
        P("mp"),
        P("mp"),
        P(),
    )
    return jax.shard_map(
        per_device, mesh=mesh, in_specs=placed, out_specs=results, check_vma=False
    )
```
